128 devices in a mesh: side: 2 (over y_hi), grp: 8 (over x, core), head: 8 (over z, y_lo).
Axes of the slice: x: 4, y: 4 (y_hi: 2, y_lo: 2; y = y_hi * 2 + y_lo), z: 4, core: 2. Of those that a mesh axis runs over, the one named last changes fastest.
Arguments:
- qkv: bfloat16 [512, 3, 4096], P(('side', 'grp'), None, 'head'), may hold values from -6 to 6
- state: float32 [512, 32, 128, 128], P(('side', 'grp'), 'head'), may hold values from -6 to 6
- decay_rate: float32 [32], P('head'), may hold values from 0.01 to 2
- attn_gain: float32 [4096], P('head'), may hold values from 0.25 to 1.75
- out_weight: bfloat16 [4096, 3072], P('head'), may hold values from -0.09375 to 0.09375
- resid: bfloat16 [512, 3072], P(('side', 'grp'), 'head'), may hold values from -6 to 6
- moe_gain: float32 [3072], P('head'), may hold values from 0.25 to 1.75
- expert_ids: int32 [512, 2], P(('side', 'grp')), may hold values from 0 to 15, all different within a row; in each aligned block of 32 rows (0 to 31, 32 to 63, ...) at most 8 rows name the same one
- gate_bins: int32 [512, 2], P(('side', 'grp')), may hold values from 1 to 15
- gate_up: bfloat16 [16, 2, 4608, 3072], P('grp', None, ('side', 'head')), may hold values from -0.109375 to 0.109375
- down: bfloat16 [16, 4608, 3072], P('grp', ('side', 'head')), may hold values from -0.09375 to 0.09375
Outputs:
- new_state: float32 [512, 32, 128, 128], P(('side', 'grp'), 'head')
- layer_out: bfloat16 [512, 3072], P(('side', 'grp'), 'head')
The draws below stay inside these ranges and needn't reach their ends.
Inputs may be any that keep to these rules, and one draw needn't show every extreme that they name: `expert_ids`: each row names 2 different experts. Among the rows of one request group (aligned blocks of 32 rows) no expert is named by more than 8 rows, a bound that some block reaches.
All inputs are finite; a program needn't handle non-finite values.
Results may differ from the reference program's by a relative error of at most 0.022.
Values may be sent and summed in bfloat16 or wider, within the bound.
No kernel may reach another device: no remote copies, remote signals or barrier semaphores. Data moves between devices by JAX's collectives and lax.ppermute only.
A program may use at most 128 MiB of HBM per device.

```python
import math
import jax
import jax.numpy as jnp
import numpy as np
from jax import lax

D = 3072
HEADS = 32
HD = 128
EXPERTS = 16
FF = 4608
TOP = 2
REQ_GRP = 32
CAP = 8
ROWS = 512


def touch_ends(values, own_key, low, largest):
    extent = values.shape
    index_at = [jax.random.randint(jax.random.fold_in(own_key, axis), (), 0, extent[axis]) for axis in range(len(extent))]
    values = values.at[tuple(index_at)].set(low)
    longest = extent.index(max(extent))
    index_at[longest] = (index_at[longest] + 1) % extent[longest]
    return values.at[tuple(index_at)].set(largest)


def shard_levels(own_key, extent, shards, least, high):
    gain = 1.0
    for dim, blocks in shards:
        heights = jax.random.uniform(jax.random.fold_in(jax.random.fold_in(own_key, 6), dim), (blocks,), jnp.float32, least / len(shards), high / len(shards))
        gain = gain * jnp.repeat(jnp.exp(heights), extent[dim] // blocks).reshape((-1,) + (1,) * (len(extent) - 1 - dim))
    return gain


def assign_block(key, own, number, rows, count, top, bound, slope):
    order = jax.random.permutation(key, count)
    heavy_load, common = load_shares(count, rows * top, bound, slope, True), load_shares(count, rows * top, bound, slope, False)
    places = jnp.arange(count)

    def named(sizes, rotation):
        used = int((sizes > 0).sum())
        fixed = max(1, used // 4)
        moved = fixed + (places - fixed + rotation * (used - fixed)) % max(1, count - fixed)
        return jnp.zeros((count,), jnp.int32).at[order[jnp.where(places < fixed, places, moved)]].set(jnp.asarray(sizes, jnp.int32))

    sizes = jnp.where(number % 4 == 0, named(heavy_load, number // 4), named(common, number - number // 4 - 1))
    mixed = jax.random.permutation(jax.random.fold_in(own, 3), count)
    donor, receiver = mixed[0:count // 2 * 2:2], mixed[1:count // 2 * 2:2]
    room = jnp.minimum(sizes[donor] - 1, bound - sizes[receiver]) // 2
    room = jnp.where((donor == order[0]) | (receiver == order[0]) | (sizes[receiver] == 0), 0, jnp.maximum(room, 0))
    moved = jax.random.randint(jax.random.fold_in(own, 4), (count // 2,), 0, 1 << 20) % (room + 1)
    sizes = sizes.at[donor].add(-moved).at[receiver].add(moved)
    labels = jnp.searchsorted(jnp.cumsum(sizes), jnp.arange(rows * top), side="right").astype(jnp.int32)
    table = labels.reshape(top, rows).T
    table = table[jax.random.permutation(jax.random.fold_in(own, 1), rows)]
    rotation = jax.random.randint(jax.random.fold_in(own, 2), (rows, 1), 0, top)
    return jnp.take_along_axis(table, (jnp.arange(top)[None, :] + rotation) % top, axis=1)


def load_shares(number_of, total, bound, slope, full):
    portions = [(1 << 20) // math.isqrt(standing ** slope) + 1 for standing in range(1, number_of + 1)]
    largest = bound if full else min(bound, max(-(-total // number_of), total * portions[0] // sum(portions)))
    least = 1 if total - largest >= number_of - 1 else 0
    holding, rest = [largest] + [least] * (number_of - 1), total - largest - least * (number_of - 1)
    while rest > 0:
        free = [i for i in range(1, number_of) if holding[i] < largest] or [i for i in range(1, number_of) if holding[i] < bound]
        whole, remaining = sum([portions[i] for i in free]), rest
        for i in free:
            addition = min(bound - holding[i], max(1, remaining * portions[i] // whole), rest)
            holding[i] = holding[i] + addition
            rest = rest - addition
    return np.array(holding)


def centred(stream_key, dims, deviation, most, pieces=(), kind=jnp.bfloat16):
    gain = shard_levels(stream_key, dims, pieces, -0.22, 0.18) if pieces else 1.0
    result = jax.random.normal(stream_key, dims, jnp.float32) * deviation * gain
    return jnp.minimum(jnp.maximum(result, -most), most).astype(kind)


def setup_inputs(seed: int = 0) -> dict:
    key_list = jax.random.split(jax.random.key(seed), 12)
    qkv = centred(key_list[0], (ROWS, 3, HEADS * HD), 1.0, 6.0, ((0, 16), (2, 8)))
    state = centred(key_list[1], (ROWS, HEADS, HD, HD), 1.0, 6.0, ((0, 16), (1, 8)), jnp.float32)
    decay_rate = jnp.clip(jnp.exp(math.log(2.0) - 5.2983174 * jax.random.uniform(key_list[2], (HEADS,), jnp.float32) ** shard_levels(key_list[2], (HEADS,), ((0, 8),), -0.2, 0.2)), 0.01, 2.0)
    attn_gain = jnp.clip(1.0 + 0.15 * jax.random.normal(key_list[3], (HEADS * HD,), jnp.float32), 0.25, 1.75)
    out_weight = centred(key_list[4], (HEADS * HD, D), (HEADS * HD) ** -0.5, 0.09375, ((0, 8),))
    resid = centred(key_list[5], (ROWS, D), 1.0, 6.0, ((0, 16), (1, 8)))
    moe_gain = jnp.clip(1.0 + 0.15 * jax.random.normal(key_list[6], (D,), jnp.float32), 0.25, 1.75)
    expert_ids_keys = jax.random.split(jax.random.fold_in(key_list[7], 1), ROWS // REQ_GRP)
    expert_ids_turns = jax.random.permutation(jax.random.fold_in(key_list[7], 3), ROWS // REQ_GRP)
    expert_ids = jax.vmap(lambda own, number: assign_block(jax.random.fold_in(key_list[7], 2), own, number, REQ_GRP, EXPERTS, TOP, CAP, 2))(expert_ids_keys, expert_ids_turns).reshape((ROWS, TOP))
    gate_bins = touch_ends(jax.random.randint(key_list[8], (ROWS, TOP), 1, 16), jax.random.fold_in(key_list[8], 1), 1, 15).astype(jnp.int32)
    gate_up = centred(key_list[9], (EXPERTS, 2, FF, D), D ** -0.5, 0.109375, ((0, 8), (2, 16)))
    down = centred(key_list[10], (EXPERTS, FF, D), FF ** -0.5, 0.09375, ((0, 8), (1, 16)))
    return {"qkv": qkv, "state": state, "decay_rate": decay_rate, "attn_gain": attn_gain, "out_weight": out_weight, "resid": resid, "moe_gain": moe_gain, "expert_ids": expert_ids, "gate_bins": gate_bins, "gate_up": gate_up, "down": down}


EPS = 1e-06

def reference(qkv, state, decay_rate, attn_gain, out_weight, resid, moe_gain, expert_ids, gate_bins, gate_up, down):
    row_count = qkv.shape[0]
    queries = qkv[:, 0].astype(jnp.float32).reshape(row_count, HEADS, HD)
    keys_vec = qkv[:, 1].astype(jnp.float32).reshape(row_count, HEADS, HD)
    values_vec = qkv[:, 2].astype(jnp.float32).reshape(row_count, HEADS, HD)
    retain = jnp.exp(-decay_rate)
    new_state = retain[None, :, None, None] * state + keys_vec[:, :, :, None] * values_vec[:, :, None, :]
    readout = jnp.einsum('rhi,rhij->rhj', queries, new_state, precision=lax.Precision.HIGHEST)
    flat_out = readout.reshape(row_count, HEADS * HD)
    mean_sq = lax.optimization_barrier(jnp.mean(flat_out * flat_out, axis=1, keepdims=True))
    normed = (flat_out * lax.rsqrt(mean_sq + EPS) * attn_gain[None, :]).astype(jnp.bfloat16)
    attn = jnp.dot(normed, out_weight, preferred_element_type=jnp.float32)
    hidden_state = resid.astype(jnp.float32) + attn
    mean_two = lax.optimization_barrier(jnp.mean(hidden_state * hidden_state, axis=1, keepdims=True))
    mixed_in = (hidden_state * lax.rsqrt(mean_two + EPS) * moe_gain[None, :]).astype(jnp.bfloat16)
    blocks = row_count // REQ_GRP
    pairs = REQ_GRP * TOP
    pair_ids = expert_ids.reshape(blocks, pairs)
    chosen = (pair_ids[:, :, None] == jnp.arange(EXPERTS, dtype=jnp.int32)[None, None, :]).astype(jnp.int32)
    earlier = (jnp.cumsum(chosen, axis=1) - chosen).astype(jnp.int32)
    position = lax.optimization_barrier(jnp.sum(earlier * chosen, axis=2)).astype(jnp.int32)
    slot_ids = (pair_ids * CAP + position).astype(jnp.int32)
    placing = (slot_ids[:, :, None] == jnp.arange(EXPERTS * CAP, dtype=jnp.int32)[None, None, :]).astype(jnp.float32)
    pair_in = jnp.repeat(mixed_in.astype(jnp.float32), TOP, axis=0).reshape(blocks, pairs, D)
    slots_in = jnp.einsum('bps,bpd->bsd', placing, pair_in, precision=lax.Precision.HIGHEST)
    slots_in = slots_in.reshape(blocks, EXPERTS, CAP, D).transpose(1, 0, 2, 3)
    slots_in = slots_in.reshape(EXPERTS, blocks * CAP, D).astype(jnp.bfloat16)

    def run_expert(operands):
        rows_in, gate_mat, down_mat = operands
        gate_act = jnp.dot(rows_in, gate_mat[0].T, preferred_element_type=jnp.float32)
        up_act = jnp.dot(rows_in, gate_mat[1].T, preferred_element_type=jnp.float32)
        activated = (jax.nn.silu(gate_act) * up_act).astype(jnp.bfloat16)
        return jnp.dot(activated, down_mat, preferred_element_type=jnp.float32).astype(jnp.bfloat16)
    slot_out = lax.map(run_expert, (slots_in, gate_up, down))
    slot_out = slot_out.reshape(EXPERTS, blocks, CAP, D).transpose(1, 0, 2, 3)
    slot_out = slot_out.reshape(blocks, EXPERTS * CAP, D).astype(jnp.float32)
    pair_out = jnp.einsum('bps,bsd->bpd', placing, slot_out, precision=lax.Precision.HIGHEST)
    pair_out = pair_out.reshape(row_count, TOP, D)
    bin_values = gate_bins.astype(jnp.float32)
    route_weight = bin_values / lax.optimization_barrier(jnp.sum(bin_values, axis=1, keepdims=True))
    layer_out = hidden_state + lax.optimization_barrier(jnp.sum(route_weight[:, :, None] * pair_out, axis=1))
    return (new_state, layer_out.astype(jnp.bfloat16))
```

```python
import functools

import jax
import jax.numpy as jnp
from jax import lax
from jax.experimental import pallas as pl
from jax.experimental.pallas import tpu as pltpu
from jax.sharding import PartitionSpec as P

CAP = 8
EPS = 1e-06
LANES = 128
ROW_CHUNK = 16
F32 = jnp.float32
BF16 = jnp.bfloat16
VMEM_LIMIT = 48 * 1024 * 1024


def split_terms(value):
    first = value.astype(BF16).astype(F32)
    rest = value - first
    second = rest.astype(BF16).astype(F32)
    third = (rest - second).astype(BF16).astype(F32)
    return first, second, third


def attention_kernel(
    decay_ref, qkv_ref, state_ref, attn_gain_ref, weight_ref, moe_gain_ref,
    new_state_ref, out_ref, acc_ref, flat_ref, square_ref, queries_ref, keys_ref, *, width,
):
    head, chunk = pl.program_id(0), pl.program_id(1)
    heads, chunks = pl.num_programs(0), pl.num_programs(1)
    rows = flat_ref.shape[0]

    @pl.when(chunk == 0)
    def _():
        queries_ref[...] = qkv_ref[:, 0, :].astype(F32).T
        keys_ref[...] = qkv_ref[:, 1, :].astype(F32).T

    retain = jnp.exp(jnp.full((1, LANES), -decay_ref[head], F32))
    for part in range(rows // ROW_CHUNK):

        @pl.when(chunk == part)
        def _():
            for i in range(ROW_CHUNK):
                row = part * ROW_CHUNK + i
                values = qkv_ref[row, 2:3, :].astype(F32)
                fresh = retain * state_ref[i, 0] + keys_ref[:, row : row + 1] * values
                new_state_ref[i, 0] = fresh
                flat_ref[row : row + 1, :] = jnp.sum(
                    queries_ref[:, row : row + 1] * fresh, axis=0, keepdims=True
                )

    @pl.when(chunk == chunks - 1)
    def _():
        flat = flat_ref[...]
        squares = jnp.sum(flat * flat, axis=1, keepdims=True)
        scaled = (flat * attn_gain_ref[...]).astype(BF16)
        term = jnp.dot(scaled, weight_ref[...], preferred_element_type=F32)

        @pl.when(head == 0)
        def _():
            square_ref[...] = jnp.broadcast_to(squares, square_ref.shape)
            acc_ref[...] = term

        @pl.when(head > 0)
        def _():
            square_ref[...] += squares
            acc_ref[...] += term

    @pl.when((chunk == chunks - 1) & (head == heads - 1))
    def _():
        square_row = square_ref[...].T[0:1, :]
        square_row = jnp.concatenate(
            [square_row, jnp.zeros((1, LANES - rows), F32)], axis=1
        )
        gain = moe_gain_ref[...]
        pieces = list(split_terms(square_row))
        for j in range(width // LANES):
            pieces += list(split_terms(gain[:, j * LANES : (j + 1) * LANES]))
        pieces.append(jnp.zeros((rows - len(pieces), LANES), F32))
        beside = jnp.concatenate(pieces, axis=0).astype(BF16)
        for target in range(out_ref.shape[0]):
            out_ref[target, :, :width] = acc_ref[
                :, target * width : (target + 1) * width
            ].astype(BF16)
            out_ref[target, :, width:] = beside


def slot_masks(ids, rows, slots):
    lane = lax.broadcasted_iota(jnp.int32, (rows, slots), 1)
    expert, place = lane // CAP, lane % CAP
    named = [(ids[:, c : c + 1] == expert) for c in range(ids.shape[1])]
    total = sum(n.astype(F32) for n in named)
    before = (
        lax.broadcasted_iota(jnp.int32, (rows, rows), 1)
        < lax.broadcasted_iota(jnp.int32, (rows, rows), 0)
    ).astype(BF16)
    earlier = jnp.dot(before, total.astype(BF16), preferred_element_type=F32)
    here = earlier == place.astype(F32)
    return [(n & here).astype(F32) for n in named]


def dispatch_kernel(
    parts_ref, resid_ref, ids_ref, out_ref, hidden_ref, gain_ref, *, features, slots,
):
    sources, rows, _ = parts_ref.shape
    width = resid_ref.shape[1]
    total = jnp.zeros((rows, width), F32)
    beside = jnp.zeros((1, LANES), F32)
    for s in range(sources):
        total += parts_ref[s, :, :width].astype(F32)
        extra = parts_ref[s, :, width:].astype(F32)
        beside += jnp.sum(extra[0:3], axis=0, keepdims=True)
        for j in range(width // LANES):
            gain_ref[:, s * width + j * LANES : s * width + (j + 1) * LANES] = jnp.sum(
                extra[3 + 3 * j : 6 + 3 * j], axis=0, keepdims=True
            )
    squares = jnp.broadcast_to(beside, (LANES, LANES)).T[:rows, 0:1]
    hidden = resid_ref[...].astype(F32) + total * lax.rsqrt(squares / features + EPS)
    hidden_ref[...] = hidden
    placing = sum(slot_masks(ids_ref[...], rows, slots)).astype(BF16)
    buckets = lax.dot_general(
        placing, hidden.astype(BF16), (((0,), (0,)), ((), ())), preferred_element_type=F32
    ).astype(BF16)
    side, grp, head, per_target, _ = out_ref.shape
    for g in range(grp):
        block = buckets[g * per_target : (g + 1) * per_target]
        for s in range(side):
            for h in range(head):
                out_ref[s, g, h] = block


def expert_kernel(
    rows_ref, gain_ref, gate_up_hbm, down_hbm, out_ref, gate_up_ref, down_ref, mixed_ref, held_ref,
    gate_up_sem, down_sem,
):
    experts = gate_up_hbm.shape[0]
    side, grp, head, per_target, width = rows_ref.shape
    model = head * width
    count = side * grp * CAP
    loads = []
    for e in range(experts):
        load_gate = pltpu.make_async_copy(gate_up_hbm.at[e], gate_up_ref.at[e], gate_up_sem.at[e])
        load_down = pltpu.make_async_copy(down_hbm.at[e], down_ref.at[e], down_sem.at[e])
        load_gate.start()
        load_down.start()
        loads.append((load_gate, load_down))

    squares = jnp.zeros((side * grp, per_target, 1), F32)
    for h in range(head):
        rows = rows_ref[:, :, h].reshape(side * grp, per_target, width).astype(F32)
        squares += jnp.sum(rows * rows, axis=2, keepdims=True)
        mixed = rows * gain_ref[:, h * width : (h + 1) * width].reshape(1, 1, width)
        for e in range(experts):
            mixed_ref[e, :, h * width : (h + 1) * width] = (
                mixed[:, e * CAP : (e + 1) * CAP].reshape(count, width).astype(BF16)
            )
    scale = lax.rsqrt(squares / model + EPS)
    for e in range(experts):
        row_scale = scale[:, e * CAP : (e + 1) * CAP].reshape(count, 1)
        loads[e][0].wait()
        contract = (((1,), (1,)), ((), ()))
        gate = row_scale * lax.dot_general(
            mixed_ref[e], gate_up_ref[e, 0], contract, preferred_element_type=F32
        )
        up = row_scale * lax.dot_general(
            mixed_ref[e], gate_up_ref[e, 1], contract, preferred_element_type=F32
        )
        activated = (gate / (1.0 + jnp.exp(-gate)) * up).astype(BF16)
        loads[e][1].wait()
        for h in range(head):
            held_ref[:, h, e * CAP : (e + 1) * CAP, :] = jnp.dot(
                activated,
                down_ref[e, :, h * width : (h + 1) * width],
                preferred_element_type=F32,
            ).reshape(side * grp, CAP, width)
    for s in range(side):
        out_ref[s] = held_ref[s * grp : (s + 1) * grp].astype(BF16)


def combine_kernel(parts_ref, hidden_ref, ids_ref, bins_ref, out_ref):
    side, grp, head, per_target, width = parts_ref.shape
    rows = hidden_ref.shape[0]
    total = jnp.zeros((grp, per_target, width), F32)
    for s in range(side):
        for h in range(head):
            total += parts_ref[s, :, h].astype(F32)
    slots = grp * per_target
    expert_out = total.reshape(slots, width).astype(BF16)
    bins = bins_ref[...].astype(F32)
    weight = bins / jnp.sum(bins, axis=1, keepdims=True)
    routed = jnp.zeros((rows, width), F32)
    for c, mask in enumerate(slot_masks(ids_ref[...], rows, slots)):
        picked = jnp.dot(mask.astype(BF16), expert_out, preferred_element_type=F32)
        routed += weight[:, c : c + 1] * picked
    out_ref[...] = (hidden_ref[...] + routed).astype(BF16)


def on_device(
    qkv, state, decay_rate, attn_gain, out_weight, resid, moe_gain, expert_ids, gate_bins,
    gate_up, down,
):
    rows, heads, head_dim, _ = state.shape
    side, grp, head = lax.axis_size("side"), lax.axis_size("grp"), lax.axis_size("head")
    width = resid.shape[1]
    model = width * head
    experts = gate_up.shape[0]
    slots = experts * grp * CAP
    vmem = pl.BlockSpec(memory_space=pltpu.VMEM)
    params = pltpu.CompilerParams(vmem_limit_bytes=VMEM_LIMIT)
    new_state, partial = pl.pallas_call(
        functools.partial(attention_kernel, width=width),
        grid=(heads, rows // ROW_CHUNK),
        in_specs=[
            pl.BlockSpec(memory_space=pltpu.SMEM),
            pl.BlockSpec((rows, 3, head_dim), lambda h, r: (0, 0, h)),
            pl.BlockSpec((ROW_CHUNK, 1, head_dim, head_dim), lambda h, r: (r, h, 0, 0)),
            pl.BlockSpec((1, head_dim), lambda h, r: (0, h)),
            pl.BlockSpec((head_dim, model), lambda h, r: (h, 0)),
            pl.BlockSpec((1, width), lambda h, r: (0, 0)),
        ],
        out_specs=[
            pl.BlockSpec((ROW_CHUNK, 1, head_dim, head_dim), lambda h, r: (r, h, 0, 0)),
            pl.BlockSpec((head, rows, width + LANES), lambda h, r: (0, 0, 0)),
        ],
        out_shape=[
            jax.ShapeDtypeStruct(state.shape, F32),
            jax.ShapeDtypeStruct((head, rows, width + LANES), BF16),
        ],
        scratch_shapes=[
            pltpu.VMEM((rows, model), F32),
            pltpu.VMEM((rows, head_dim), F32),
            pltpu.VMEM((rows, LANES), F32),
            pltpu.VMEM((head_dim, rows), F32),
            pltpu.VMEM((head_dim, rows), F32),
        ],
        compiler_params=params,
        name="attention",
    )(decay_rate, qkv, state, attn_gain[None], out_weight, moe_gain[None])
    parts = lax.all_to_all(partial, "head", 0, 0, tiled=True)

    outgoing, hidden, gain = pl.pallas_call(
        functools.partial(dispatch_kernel, features=heads * head_dim * head, slots=slots),
        in_specs=[vmem] * 3,
        out_specs=[vmem] * 3,
        out_shape=[
            jax.ShapeDtypeStruct((side, grp, head, experts * CAP, width), BF16),
            jax.ShapeDtypeStruct((rows, width), F32),
            jax.ShapeDtypeStruct((1, model), F32),
        ],
        compiler_params=params,
        name="dispatch",
    )(parts, resid, expert_ids)
    everyone = ("side", "grp", "head")
    block = (side * grp * head, experts * CAP, width)
    arrived = lax.all_to_all(outgoing.reshape(block), everyone, 0, 0, tiled=True)

    expert_out = pl.pallas_call(
        expert_kernel,
        in_specs=[vmem, vmem, pl.BlockSpec(memory_space=pl.ANY), pl.BlockSpec(memory_space=pl.ANY)],
        out_specs=vmem,
        out_shape=jax.ShapeDtypeStruct((side, grp, head, experts * CAP, width), BF16),
        scratch_shapes=[
            pltpu.VMEM(gate_up.shape, BF16),
            pltpu.VMEM(down.shape, BF16),
            pltpu.VMEM((experts, side * grp * CAP, model), BF16),
            pltpu.VMEM((side * grp, head, experts * CAP, width), F32),
            pltpu.SemaphoreType.DMA((experts,)),
            pltpu.SemaphoreType.DMA((experts,)),
        ],
        compiler_params=params,
        name="experts",
    )(arrived.reshape(side, grp, head, experts * CAP, width), gain, gate_up, down)
    returned = lax.all_to_all(expert_out.reshape(block), everyone, 0, 0, tiled=True)

    layer_out = pl.pallas_call(
        combine_kernel,
        in_specs=[vmem] * 4,
        out_specs=vmem,
        out_shape=jax.ShapeDtypeStruct((rows, width), BF16),
        compiler_params=params,
        name="combine",
    )(returned.reshape(side, grp, head, experts * CAP, width), hidden, expert_ids, gate_bins)
    return new_state, layer_out


def solution(mesh):
    placed = (
        P(("side", "grp"), None, "head"),
        P(("side", "grp"), "head", None, None),
        P("head"),
        P("head"),
        P("head", None),
        P(("side", "grp"), "head"),
        P("head"),
        P(("side", "grp"), None),
        P(("side", "grp"), None),
        P("grp", None, ("side", "head"), None),
        P("grp", ("side", "head"), None),
    )
    return jax.shard_map(
        on_device,
        mesh=mesh,
        in_specs=placed,
        out_specs=(P(("side", "grp"), "head", None, None), P(("side", "grp"), "head")),
        check_vma=False,
    )
```

```python
import functools

import jax
import jax.numpy as jnp
from jax import lax
from jax.experimental import pallas as pl
from jax.experimental.pallas import tpu as pltpu
from jax.sharding import PartitionSpec as P

CAP = 8
EPS = 1e-06
LANES = 128
IN_FLIGHT = 4
F32 = jnp.float32
BF16 = jnp.bfloat16
MIB = 1024 * 1024


def split_terms(value):
    first = value.astype(BF16).astype(F32)
    rest = value - first
    second = rest.astype(BF16).astype(F32)
    third = (rest - second).astype(BF16).astype(F32)
    return first, second, third


def row_pair_mask(row, rows, dim):
    i = lax.broadcasted_iota(jnp.int32, (rows, 2 * dim), 0)
    j = lax.broadcasted_iota(jnp.int32, (rows, 2 * dim), 1)
    return i == row + (j >= dim).astype(jnp.int32)


def readout_kernel(
    decay_ref, qkv_hbm, state_hbm, attn_gain_ref, weight_hbm, moe_gain_ref, resid_ref,
    out_ref, held_resid_ref, qkv_ref, state_ref, weight_ref, raw_ref, acc_ref, qkv_sem, state_sem, weight_sem,
):
    rows, heads, dim, _ = state_ref.shape
    width = moe_gain_ref.shape[0]
    load_qkv = pltpu.make_async_copy(qkv_hbm, qkv_ref, qkv_sem.at[0])
    load_qkv.start()
    loads = []
    for h in range(heads):
        span = pl.ds(h * dim, dim)
        loads.append(
            pltpu.make_async_copy(state_hbm.at[:, h], state_ref.at[:, h], state_sem.at[h])
        )
        loads.append(
            pltpu.make_async_copy(weight_hbm.at[span], weight_ref.at[span], weight_sem.at[h])
        )
    for load in loads[:IN_FLIGHT]:
        load.start()

    def arrive(index):
        loads[index].wait()
        if index + IN_FLIGHT < len(loads):
            loads[index + IN_FLIGHT].start()

    held_resid_ref[...] = resid_ref[...]
    masks = [row_pair_mask(row, rows, dim).astype(BF16) for row in range(0, rows, 2)]
    squares = jnp.zeros((rows, 1), F32)
    load_qkv.wait()
    for h in range(heads):
        lanes = slice(h * dim, (h + 1) * dim)
        queries, keys, values = [qkv_ref[t, :, lanes].astype(F32) for t in range(3)]
        columns = queries.T.astype(BF16)
        arrive(2 * h)
        for row in range(0, rows, 2):
            spread = jnp.dot(columns, masks[row // 2], preferred_element_type=F32)
            for u in range(2):
                raw_ref[row + u : row + u + 1, :] = jnp.sum(
                    spread[:, u * dim : (u + 1) * dim] * state_ref[row + u, h],
                    axis=0, keepdims=True,
                )
        retain = jnp.exp(jnp.full((1, dim), -decay_ref[h], F32))
        flat = retain * raw_ref[...] + jnp.sum(queries * keys, axis=1, keepdims=True) * values
        squares += jnp.sum(flat * flat, axis=1, keepdims=True)
        scaled = (flat * attn_gain_ref[lanes].reshape(1, dim)).astype(BF16)
        arrive(2 * h + 1)
        term = jnp.dot(scaled, weight_ref[lanes, :], preferred_element_type=F32)
        if h == 0:
            acc_ref[...] = term
        else:
            acc_ref[...] += term

    square_row = jnp.broadcast_to(squares, (rows, LANES)).T[0:1, :]
    square_row = jnp.concatenate([square_row, jnp.zeros((1, LANES - rows), F32)], axis=1)
    pieces = list(split_terms(square_row))
    for j in range(width // LANES):
        pieces += list(split_terms(moe_gain_ref[j * LANES : (j + 1) * LANES].reshape(1, LANES)))
    pieces.append(jnp.zeros((rows - len(pieces), LANES), F32))
    beside = jnp.concatenate(pieces, axis=0).astype(BF16)
    for target in range(out_ref.shape[0]):
        out_ref[target, :, :width] = acc_ref[:, target * width : (target + 1) * width].astype(BF16)
        out_ref[target, :, width:] = beside


def update_kernel(decay_ref, qkv_ref, state_ref, after_ref, out_ref):
    del after_ref
    head = pl.program_id(0)
    rows, dim = qkv_ref.shape[1:]
    columns = qkv_ref[1].astype(F32).T.astype(BF16)
    values = qkv_ref[2].astype(F32)
    values = jnp.concatenate([values, values], axis=1)
    retain = jnp.exp(jnp.full((1, dim), -decay_ref[head], F32))
    for row in range(0, rows, 2):
        picked = jnp.where(row_pair_mask(row, rows, dim), values, 0.0).astype(BF16)
        outer = jnp.dot(columns, picked, preferred_element_type=F32)
        for u in range(2):
            out_ref[row + u, 0] = (
                retain * state_ref[row + u, 0] + outer[:, u * dim : (u + 1) * dim]
            )


def slot_masks(ids, rows, slots):
    lane = lax.broadcasted_iota(jnp.int32, (rows, slots), 1)
    expert, place = lane // CAP, lane % CAP
    named = [(ids[:, c : c + 1] == expert) for c in range(ids.shape[1])]
    total = sum(n.astype(F32) for n in named)
    before = (
        lax.broadcasted_iota(jnp.int32, (rows, rows), 1)
        < lax.broadcasted_iota(jnp.int32, (rows, rows), 0)
    ).astype(BF16)
    earlier = jnp.dot(before, total.astype(BF16), preferred_element_type=F32)
    here = earlier == place.astype(F32)
    return [(n & here).astype(F32) for n in named]


def dispatch_kernel(
    parts_ref, resid_ref, ids_ref, out_ref, hidden_ref, gain_ref, *, features, slots,
):
    sources, rows, _ = parts_ref.shape
    width = resid_ref.shape[1]
    total = jnp.zeros((rows, width), F32)
    beside = jnp.zeros((1, LANES), F32)
    for s in range(sources):
        total += parts_ref[s, :, :width].astype(F32)
        extra = parts_ref[s, :, width:].astype(F32)
        beside += jnp.sum(extra[0:3], axis=0, keepdims=True)
        for j in range(width // LANES):
            gain_ref[:, s * width + j * LANES : s * width + (j + 1) * LANES] = jnp.sum(
                extra[3 + 3 * j : 6 + 3 * j], axis=0, keepdims=True
            )
    squares = jnp.broadcast_to(beside, (LANES, LANES)).T[:rows, 0:1]
    hidden = resid_ref[...].astype(F32) + total * lax.rsqrt(squares / features + EPS)
    hidden_ref[...] = hidden
    placing = sum(slot_masks(ids_ref[...], rows, slots)).astype(BF16)
    buckets = lax.dot_general(
        placing, hidden.astype(BF16), (((0,), (0,)), ((), ())), preferred_element_type=F32
    ).astype(BF16)
    side, grp, head, per_target, _ = out_ref.shape
    for g in range(grp):
        block = buckets[g * per_target : (g + 1) * per_target]
        for s in range(side):
            for h in range(head):
                out_ref[s, g, h] = block


def expert_kernel(
    rows_ref, gain_ref, gate_up_hbm, down_hbm, out_ref,
    gate_up_ref, down_ref, mixed_ref, held_ref, gate_up_sem, down_sem,
):
    experts = gate_up_hbm.shape[0]
    side, grp, head, per_target, width = rows_ref.shape
    model = head * width
    count = side * grp * CAP
    loads = []
    for e in range(experts):
        loads.append(
            (
                pltpu.make_async_copy(gate_up_hbm.at[e], gate_up_ref.at[e], gate_up_sem.at[e]),
                pltpu.make_async_copy(down_hbm.at[e], down_ref.at[e], down_sem.at[e]),
            )
        )
    loads[0][0].start()

    squares = jnp.zeros((side * grp, per_target, 1), F32)
    for h in range(head):
        rows = rows_ref[:, :, h].reshape(side * grp, per_target, width).astype(F32)
        squares += jnp.sum(rows * rows, axis=2, keepdims=True)
        mixed = rows * gain_ref[:, h * width : (h + 1) * width].reshape(1, 1, width)
        for e in range(experts):
            mixed_ref[e, :, h * width : (h + 1) * width] = (
                mixed[:, e * CAP : (e + 1) * CAP].reshape(count, width).astype(BF16)
            )
    scale = lax.rsqrt(squares / model + EPS)
    contract = (((1,), (1,)), ((), ()))
    for e in range(experts):
        row_scale = scale[:, e * CAP : (e + 1) * CAP].reshape(count, 1)
        if e == 0:
            loads[0][1].start()
            for i in range(1, experts):
                loads[i][0].start()
            loads[0][0].wait()
            for i in range(1, experts):
                loads[i][1].start()
        gate = row_scale * lax.dot_general(
            mixed_ref[e], gate_up_ref[e, 0], contract, preferred_element_type=F32
        )
        up = row_scale * lax.dot_general(
            mixed_ref[e], gate_up_ref[e, 1], contract, preferred_element_type=F32
        )
        activated = (gate / (1.0 + jnp.exp(-gate)) * up).astype(BF16)
        loads[e][1].wait()
        if e == 0:
            for i in range(1, experts):
                loads[i][0].wait()
        for h in range(head):
            held_ref[:, h, e * CAP : (e + 1) * CAP, :] = jnp.dot(
                activated,
                down_ref[e, :, h * width : (h + 1) * width],
                preferred_element_type=F32,
            ).reshape(side * grp, CAP, width)
    for s in range(side):
        out_ref[s] = held_ref[s * grp : (s + 1) * grp].astype(BF16)


def combine_kernel(parts_ref, hidden_ref, ids_ref, bins_ref, out_ref):
    side, grp, head, per_target, width = parts_ref.shape
    rows = hidden_ref.shape[0]
    total = jnp.zeros((grp, per_target, width), F32)
    for s in range(side):
        for h in range(head):
            total += parts_ref[s, :, h].astype(F32)
    slots = grp * per_target
    expert_out = total.reshape(slots, width).astype(BF16)
    bins = bins_ref[...].astype(F32)
    weight = bins / jnp.sum(bins, axis=1, keepdims=True)
    routed = jnp.zeros((rows, width), F32)
    for c, mask in enumerate(slot_masks(ids_ref[...], rows, slots)):
        picked = jnp.dot(mask.astype(BF16), expert_out, preferred_element_type=F32)
        routed += weight[:, c : c + 1] * picked
    out_ref[...] = (hidden_ref[...] + routed).astype(BF16)


def in_hbm(*arrays):
    return [pltpu.with_memory_space_constraint(array, pltpu.HBM) for array in arrays]


def on_device(
    qkv, state, decay_rate, attn_gain, out_weight, resid, moe_gain, expert_ids, gate_bins,
    gate_up, down,
):
    rows, heads, head_dim, _ = state.shape
    side, grp, head = lax.axis_size("side"), lax.axis_size("grp"), lax.axis_size("head")
    width = resid.shape[1]
    model = width * head
    experts = gate_up.shape[0]
    slots = experts * grp * CAP
    vmem, hbm = pl.BlockSpec(memory_space=pltpu.VMEM), pl.BlockSpec(memory_space=pltpu.HBM)
    smem = pl.BlockSpec(memory_space=pltpu.SMEM)
    params = pltpu.CompilerParams(vmem_limit_bytes=24 * MIB)
    qkv = jnp.transpose(qkv, (1, 0, 2))
    partial, held_resid = pl.pallas_call(
        readout_kernel,
        in_specs=[smem, hbm, hbm, vmem, hbm, vmem, vmem],
        out_specs=[vmem, vmem],
        out_shape=[
            jax.ShapeDtypeStruct((head, rows, width + LANES), BF16),
            jax.ShapeDtypeStruct((rows, width), BF16),
        ],
        scratch_shapes=[
            pltpu.VMEM(qkv.shape, BF16),
            pltpu.VMEM(state.shape, F32),
            pltpu.VMEM(out_weight.shape, BF16),
            pltpu.VMEM((rows, head_dim), F32),
            pltpu.VMEM((rows, model), F32),
            pltpu.SemaphoreType.DMA((1,)),
            pltpu.SemaphoreType.DMA((heads,)),
            pltpu.SemaphoreType.DMA((heads,)),
        ],
        compiler_params=params,
        name="readout",
    )(
        *in_hbm(decay_rate, qkv, state, attn_gain, out_weight, moe_gain, resid)
    )
    parts = lax.all_to_all(partial, "head", 0, 0, tiled=True)

    outgoing, hidden, gain = pl.pallas_call(
        functools.partial(dispatch_kernel, features=heads * head_dim * head, slots=slots),
        in_specs=[vmem] * 3,
        out_specs=[vmem] * 3,
        out_shape=[
            jax.ShapeDtypeStruct((side, grp, head, experts * CAP, width), BF16),
            jax.ShapeDtypeStruct((rows, width), F32),
            jax.ShapeDtypeStruct((1, model), F32),
        ],
        compiler_params=params,
        name="dispatch",
    )(parts, held_resid, expert_ids)
    everyone = ("side", "grp", "head")
    block = (side * grp * head, experts * CAP, width)
    arrived = lax.all_to_all(outgoing.reshape(block), everyone, 0, 0, tiled=True)

    new_state = pl.pallas_call(
        update_kernel,
        grid=(heads,),
        in_specs=[
            smem,
            pl.BlockSpec((3, rows, head_dim), lambda h: (0, 0, h)),
            pl.BlockSpec((rows, 1, head_dim, head_dim), lambda h: (0, h, 0, 0)),
            pl.BlockSpec(memory_space=pl.ANY),
        ],
        out_specs=pl.BlockSpec((rows, 1, head_dim, head_dim), lambda h: (0, h, 0, 0)),
        out_shape=jax.ShapeDtypeStruct(state.shape, F32),
        compiler_params=params,
        cost_estimate=pl.CostEstimate(
            flops=4 * state.size, bytes_accessed=8 * state.size, transcendentals=0
        ),
        name="update",
    )(*in_hbm(decay_rate, qkv, state), hidden)

    expert_out = pl.pallas_call(
        expert_kernel,
        in_specs=[vmem, vmem, hbm, hbm],
        out_specs=vmem,
        out_shape=jax.ShapeDtypeStruct((side, grp, head, experts * CAP, width), BF16),
        scratch_shapes=[
            pltpu.VMEM(gate_up.shape, BF16),
            pltpu.VMEM(down.shape, BF16),
            pltpu.VMEM((experts, side * grp * CAP, model), BF16),
            pltpu.VMEM((side * grp, head, experts * CAP, width), F32),
            pltpu.SemaphoreType.DMA((experts,)),
            pltpu.SemaphoreType.DMA((experts,)),
        ],
        compiler_params=pltpu.CompilerParams(vmem_limit_bytes=32 * MIB),
        name="experts",
    )(
        arrived.reshape(side, grp, head, experts * CAP, width), gain,
        *in_hbm(gate_up, down),
    )
    returned = lax.all_to_all(expert_out.reshape(block), everyone, 0, 0, tiled=True)

    layer_out = pl.pallas_call(
        combine_kernel,
        in_specs=[vmem] * 4,
        out_specs=vmem,
        out_shape=jax.ShapeDtypeStruct((rows, width), BF16),
        compiler_params=params,
        name="combine",
    )(returned.reshape(side, grp, head, experts * CAP, width), hidden, expert_ids, gate_bins)
    return new_state, layer_out


def solution(mesh):
    placed = (
        P(("side", "grp"), None, "head"),
        P(("side", "grp"), "head", None, None),
        P("head"),
        P("head"),
        P("head", None),
        P(("side", "grp"), "head"),
        P("head"),
        P(("side", "grp"), None),
        P(("side", "grp"), None),
        P("grp", None, ("side", "head"), None),
        P("grp", ("side", "head"), None),
    )
    return jax.shard_map(
        on_device,
        mesh=mesh,
        in_specs=placed,
        out_specs=(P(("side", "grp"), "head", None, None), P(("side", "grp"), "head")),
        check_vma=False,
    )
```

```python
import functools

import jax
import jax.numpy as jnp
from jax import lax
from jax.experimental import pallas as pl
from jax.experimental.pallas import tpu as pltpu
from jax.sharding import PartitionSpec as P

CAP = 8
EPS = 1e-06
LANES = 128
IN_FLIGHT = 4
F32 = jnp.float32
BF16 = jnp.bfloat16
MIB = 1024 * 1024


def split_terms(value):
    first = value.astype(BF16).astype(F32)
    rest = value - first
    second = rest.astype(BF16).astype(F32)
    third = (rest - second).astype(BF16).astype(F32)
    return first, second, third


def row_pair_mask(row, rows, dim):
    i = lax.broadcasted_iota(jnp.int32, (rows, 2 * dim), 0)
    j = lax.broadcasted_iota(jnp.int32, (rows, 2 * dim), 1)
    return i == row + (j >= dim).astype(jnp.int32)


def readout_kernel(
    decay_ref, qkv_hbm, state_hbm, attn_gain_ref, weight_hbm, moe_gain_ref, resid_ref,
    out_ref, held_resid_ref, qkv_ref, state_ref, weight_ref, raw_ref, acc_ref, qkv_sem, state_sem, weight_sem,
):
    rows, heads, dim, _ = state_ref.shape
    width = moe_gain_ref.shape[0]
    load_qkv = pltpu.make_async_copy(qkv_hbm, qkv_ref, qkv_sem.at[0])
    load_qkv.start()
    loads = []
    for h in range(heads):
        span = pl.ds(h * dim, dim)
        loads.append(
            pltpu.make_async_copy(state_hbm.at[:, h], state_ref.at[:, h], state_sem.at[h])
        )
        loads.append(
            pltpu.make_async_copy(weight_hbm.at[span], weight_ref.at[span], weight_sem.at[h])
        )
    for load in loads[:IN_FLIGHT]:
        load.start()

    def arrive(index):
        loads[index].wait()
        if index + IN_FLIGHT < len(loads):
            loads[index + IN_FLIGHT].start()

    held_resid_ref[...] = resid_ref[...]
    masks = [row_pair_mask(row, rows, dim).astype(BF16) for row in range(0, rows, 2)]
    squares = jnp.zeros((rows, 1), F32)
    load_qkv.wait()
    for h in range(heads):
        lanes = slice(h * dim, (h + 1) * dim)
        queries, keys, values = [qkv_ref[t, :, lanes].astype(F32) for t in range(3)]
        columns = queries.T.astype(BF16)
        arrive(2 * h)
        for row in range(0, rows, 2):
            spread = jnp.dot(columns, masks[row // 2], preferred_element_type=F32)
            for u in range(2):
                raw_ref[row + u : row + u + 1, :] = jnp.sum(
                    spread[:, u * dim : (u + 1) * dim] * state_ref[row + u, h],
                    axis=0, keepdims=True,
                )
        retain = jnp.exp(jnp.full((1, dim), -decay_ref[h], F32))
        flat = retain * raw_ref[...] + jnp.sum(queries * keys, axis=1, keepdims=True) * values
        squares += jnp.sum(flat * flat, axis=1, keepdims=True)
        scaled = (flat * attn_gain_ref[lanes].reshape(1, dim)).astype(BF16)
        arrive(2 * h + 1)
        term = jnp.dot(scaled, weight_ref[lanes, :], preferred_element_type=F32)
        if h == 0:
            acc_ref[...] = term
        else:
            acc_ref[...] += term

    square_row = jnp.broadcast_to(squares, (rows, LANES)).T[0:1, :]
    square_row = jnp.concatenate([square_row, jnp.zeros((1, LANES - rows), F32)], axis=1)
    pieces = list(split_terms(square_row))
    for j in range(width // LANES):
        pieces += list(split_terms(moe_gain_ref[j * LANES : (j + 1) * LANES].reshape(1, LANES)))
    pieces.append(jnp.zeros((rows - len(pieces), LANES), F32))
    beside = jnp.concatenate(pieces, axis=0).astype(BF16)
    for target in range(out_ref.shape[0]):
        out_ref[target, :, :width] = acc_ref[:, target * width : (target + 1) * width].astype(BF16)
        out_ref[target, :, width:] = beside


def update_kernel(decay_ref, qkv_ref, state_ref, after_ref, out_ref):
    del after_ref
    head = pl.program_id(0)
    rows, dim = qkv_ref.shape[1:]
    columns = qkv_ref[1].astype(F32).T.astype(BF16)
    values = qkv_ref[2].astype(F32)
    values = jnp.concatenate([values, values], axis=1)
    retain = jnp.exp(jnp.full((1, dim), -decay_ref[head], F32))
    for row in range(0, rows, 2):
        picked = jnp.where(row_pair_mask(row, rows, dim), values, 0.0).astype(BF16)
        outer = jnp.dot(columns, picked, preferred_element_type=F32)
        for u in range(2):
            out_ref[row + u, 0] = (
                retain * state_ref[row + u, 0] + outer[:, u * dim : (u + 1) * dim]
            )


def as_columns(table):
    rows = table.shape[1]
    padded = [table.astype(F32), jnp.zeros((8 - table.shape[0], rows), F32)]
    return jnp.concatenate(padded, axis=0).T


def slot_masks(table, rows, slots):
    ids = as_columns(table)
    lane = lax.broadcasted_iota(jnp.int32, (rows, slots), 1)
    expert, place = lane // CAP, lane % CAP
    named = [(ids[:, c : c + 1] == expert.astype(F32)) for c in range(table.shape[0])]
    total = sum(n.astype(F32) for n in named)
    before = (
        lax.broadcasted_iota(jnp.int32, (rows, rows), 1)
        < lax.broadcasted_iota(jnp.int32, (rows, rows), 0)
    ).astype(BF16)
    earlier = jnp.dot(before, total.astype(BF16), preferred_element_type=F32)
    here = earlier == place.astype(F32)
    return [(n & here).astype(F32) for n in named]


def dispatch_kernel(
    parts_ref, resid_ref, ids_ref, out_ref, hidden_ref, gain_ref, *, features, slots,
):
    sources, rows, _ = parts_ref.shape
    width = resid_ref.shape[1]
    total = jnp.zeros((rows, width), F32)
    beside = jnp.zeros((1, LANES), F32)
    for s in range(sources):
        total += parts_ref[s, :, :width].astype(F32)
        extra = parts_ref[s, :, width:].astype(F32)
        beside += jnp.sum(extra[0:3], axis=0, keepdims=True)
        for j in range(width // LANES):
            gain_ref[:, s * width + j * LANES : s * width + (j + 1) * LANES] = jnp.sum(
                extra[3 + 3 * j : 6 + 3 * j], axis=0, keepdims=True
            )
    squares = jnp.broadcast_to(beside, (LANES, LANES)).T[:rows, 0:1]
    hidden = resid_ref[...].astype(F32) + total * lax.rsqrt(squares / features + EPS)
    hidden_ref[...] = hidden
    placing = sum(slot_masks(ids_ref[...], rows, slots)).astype(BF16)
    buckets = lax.dot_general(
        placing, hidden.astype(BF16), (((0,), (0,)), ((), ())), preferred_element_type=F32
    ).astype(BF16)
    side, grp, head, per_target, _ = out_ref.shape
    for g in range(grp):
        block = buckets[g * per_target : (g + 1) * per_target]
        for s in range(side):
            for h in range(head):
                out_ref[s, g, h] = block


def expert_kernel(rows_ref, gain_ref, gate_up_ref, down_ref, out_ref, mixed_ref, held_ref):
    experts = gate_up_ref.shape[0]
    side, grp, head, per_target, width = rows_ref.shape
    model = head * width
    count = side * grp * CAP
    squares = jnp.zeros((side * grp, per_target, 1), F32)
    for h in range(head):
        rows = rows_ref[:, :, h].reshape(side * grp, per_target, width).astype(F32)
        squares += jnp.sum(rows * rows, axis=2, keepdims=True)
        mixed = rows * gain_ref[:, h * width : (h + 1) * width].reshape(1, 1, width)
        for e in range(experts):
            mixed_ref[e, :, h * width : (h + 1) * width] = (
                mixed[:, e * CAP : (e + 1) * CAP].reshape(count, width).astype(BF16)
            )
    scale = lax.rsqrt(squares / model + EPS)
    for e in range(experts):
        row_scale = scale[:, e * CAP : (e + 1) * CAP].reshape(count, 1)
        contract = (((1,), (1,)), ((), ()))
        gate = row_scale * lax.dot_general(
            mixed_ref[e], gate_up_ref[e, 0], contract, preferred_element_type=F32
        )
        up = row_scale * lax.dot_general(
            mixed_ref[e], gate_up_ref[e, 1], contract, preferred_element_type=F32
        )
        activated = (gate / (1.0 + jnp.exp(-gate)) * up).astype(BF16)
        for h in range(head):
            held_ref[:, h, e * CAP : (e + 1) * CAP, :] = jnp.dot(
                activated,
                down_ref[e, :, h * width : (h + 1) * width],
                preferred_element_type=F32,
            ).reshape(side * grp, CAP, width)
    for s in range(side):
        out_ref[s] = held_ref[s * grp : (s + 1) * grp].astype(BF16)


def combine_kernel(parts_ref, hidden_ref, ids_ref, bins_ref, out_ref):
    side, grp, head, per_target, width = parts_ref.shape
    rows = hidden_ref.shape[0]
    total = jnp.zeros((grp, per_target, width), F32)
    for s in range(side):
        for h in range(head):
            total += parts_ref[s, :, h].astype(F32)
    slots = grp * per_target
    expert_out = total.reshape(slots, width).astype(BF16)
    bins = as_columns(bins_ref[...])
    weight = bins / jnp.sum(bins, axis=1, keepdims=True)
    routed = jnp.zeros((rows, width), F32)
    for c, mask in enumerate(slot_masks(ids_ref[...], rows, slots)):
        picked = jnp.dot(mask.astype(BF16), expert_out, preferred_element_type=F32)
        routed += weight[:, c : c + 1] * picked
    out_ref[...] = (hidden_ref[...] + routed).astype(BF16)


def in_hbm(*arrays):
    return [pltpu.with_memory_space_constraint(array, pltpu.HBM) for array in arrays]


def on_device(
    qkv, state, decay_rate, attn_gain, out_weight, resid, moe_gain, expert_ids, gate_bins,
    gate_up, down,
):
    rows, heads, head_dim, _ = state.shape
    side, grp, head = lax.axis_size("side"), lax.axis_size("grp"), lax.axis_size("head")
    width = resid.shape[1]
    model = width * head
    experts = gate_up.shape[0]
    slots = experts * grp * CAP
    vmem, hbm = pl.BlockSpec(memory_space=pltpu.VMEM), pl.BlockSpec(memory_space=pltpu.HBM)
    smem = pl.BlockSpec(memory_space=pltpu.SMEM)
    params = pltpu.CompilerParams(vmem_limit_bytes=24 * MIB)
    qkv = jnp.transpose(qkv, (1, 0, 2))
    expert_ids, gate_bins = expert_ids.T, gate_bins.T
    partial, held_resid = pl.pallas_call(
        readout_kernel,
        in_specs=[smem, hbm, hbm, vmem, hbm, vmem, vmem],
        out_specs=[vmem, vmem],
        out_shape=[
            jax.ShapeDtypeStruct((head, rows, width + LANES), BF16),
            jax.ShapeDtypeStruct((rows, width), BF16),
        ],
        scratch_shapes=[
            pltpu.VMEM(qkv.shape, BF16),
            pltpu.VMEM(state.shape, F32),
            pltpu.VMEM(out_weight.shape, BF16),
            pltpu.VMEM((rows, head_dim), F32),
            pltpu.VMEM((rows, model), F32),
            pltpu.SemaphoreType.DMA((1,)),
            pltpu.SemaphoreType.DMA((heads,)),
            pltpu.SemaphoreType.DMA((heads,)),
        ],
        compiler_params=params,
        name="readout",
    )(
        *in_hbm(decay_rate, qkv, state, attn_gain, out_weight, moe_gain, resid)
    )
    parts = lax.all_to_all(partial, "head", 0, 0, tiled=True)

    outgoing, hidden, gain = pl.pallas_call(
        functools.partial(dispatch_kernel, features=heads * head_dim * head, slots=slots),
        in_specs=[vmem] * 3,
        out_specs=[vmem] * 3,
        out_shape=[
            jax.ShapeDtypeStruct((side, grp, head, experts * CAP, width), BF16),
            jax.ShapeDtypeStruct((rows, width), F32),
            jax.ShapeDtypeStruct((1, model), F32),
        ],
        compiler_params=params,
        name="dispatch",
    )(parts, held_resid, expert_ids)
    everyone = ("side", "grp", "head")
    block = (side * grp * head, experts * CAP, width)
    arrived = lax.all_to_all(outgoing.reshape(block), everyone, 0, 0, tiled=True)

    new_state = pl.pallas_call(
        update_kernel,
        grid=(heads,),
        in_specs=[
            smem,
            pl.BlockSpec((3, rows, head_dim), lambda h: (0, 0, h)),
            pl.BlockSpec((rows, 1, head_dim, head_dim), lambda h: (0, h, 0, 0)),
            pl.BlockSpec(memory_space=pl.ANY),
        ],
        out_specs=pl.BlockSpec((rows, 1, head_dim, head_dim), lambda h: (0, h, 0, 0)),
        out_shape=jax.ShapeDtypeStruct(state.shape, F32),
        compiler_params=params,
        cost_estimate=pl.CostEstimate(
            flops=4 * state.size, bytes_accessed=8 * state.size, transcendentals=0
        ),
        name="update",
    )(*in_hbm(decay_rate, qkv, state), hidden)

    expert_out = pl.pallas_call(
        expert_kernel,
        in_specs=[vmem] * 4,
        out_specs=vmem,
        out_shape=jax.ShapeDtypeStruct((side, grp, head, experts * CAP, width), BF16),
        scratch_shapes=[
            pltpu.VMEM((experts, side * grp * CAP, model), BF16),
            pltpu.VMEM((side * grp, head, experts * CAP, width), F32),
        ],
        compiler_params=params,
        name="experts",
    )(
        arrived.reshape(side, grp, head, experts * CAP, width), gain,
        pltpu.with_memory_space_constraint(gate_up, pltpu.VMEM),
        pltpu.with_memory_space_constraint(down, pltpu.VMEM),
    )
    returned = lax.all_to_all(expert_out.reshape(block), everyone, 0, 0, tiled=True)

    layer_out = pl.pallas_call(
        combine_kernel,
        in_specs=[vmem] * 4,
        out_specs=vmem,
        out_shape=jax.ShapeDtypeStruct((rows, width), BF16),
        compiler_params=params,
        name="combine",
    )(returned.reshape(side, grp, head, experts * CAP, width), hidden, expert_ids, gate_bins)
    return new_state, layer_out


def solution(mesh):
    placed = (
        P(("side", "grp"), None, "head"),
        P(("side", "grp"), "head", None, None),
        P("head"),
        P("head"),
        P("head", None),
        P(("side", "grp"), "head"),
        P("head"),
        P(("side", "grp"), None),
        P(("side", "grp"), None),
        P("grp", None, ("side", "head"), None),
        P("grp", ("side", "head"), None),
    )
    return jax.shard_map(
        on_device,
        mesh=mesh,
        in_specs=placed,
        out_specs=(P(("side", "grp"), "head", None, None), P(("side", "grp"), "head")),
        check_vma=False,
    )
```

```python
import functools

import jax
import jax.numpy as jnp
from jax import lax
from jax.experimental import pallas as pl
from jax.experimental.pallas import tpu as pltpu
from jax.sharding import PartitionSpec as P

CAP = 8
EPS = 1e-06
LANES = 128
IN_FLIGHT = 4
F32 = jnp.float32
BF16 = jnp.bfloat16
MIB = 1024 * 1024


def split_terms(value):
    first = value.astype(BF16).astype(F32)
    rest = value - first
    second = rest.astype(BF16).astype(F32)
    third = (rest - second).astype(BF16).astype(F32)
    return first, second, third


def row_pair_mask(row, rows, dim):
    i = lax.broadcasted_iota(jnp.int32, (rows, 2 * dim), 0)
    j = lax.broadcasted_iota(jnp.int32, (rows, 2 * dim), 1)
    return i == row + (j >= dim).astype(jnp.int32)


def readout_kernel(
    decay_ref, qkv_hbm, state_hbm, attn_gain_ref, weight_hbm, moe_gain_ref, resid_ref,
    out_ref, held_resid_ref, qkv_ref, state_ref, weight_ref, raw_ref, acc_ref, qkv_sem, state_sem, weight_sem,
):
    rows, heads, dim, _ = state_ref.shape
    width = moe_gain_ref.shape[0]
    load_qkv = pltpu.make_async_copy(qkv_hbm, qkv_ref, qkv_sem.at[0])
    load_qkv.start()
    loads = []
    for h in range(heads):
        span = pl.ds(h * dim, dim)
        loads.append(
            pltpu.make_async_copy(state_hbm.at[:, h], state_ref.at[:, h], state_sem.at[h])
        )
        loads.append(
            pltpu.make_async_copy(weight_hbm.at[span], weight_ref.at[span], weight_sem.at[h])
        )
    for load in loads[:IN_FLIGHT]:
        load.start()

    def arrive(index):
        loads[index].wait()
        if index + IN_FLIGHT < len(loads):
            loads[index + IN_FLIGHT].start()

    held_resid_ref[...] = resid_ref[...]
    masks = [row_pair_mask(row, rows, dim).astype(BF16) for row in range(0, rows, 2)]
    squares = jnp.zeros((rows, 1), F32)
    load_qkv.wait()
    for h in range(heads):
        lanes = slice(h * dim, (h + 1) * dim)
        queries, keys, values = [qkv_ref[t, :, lanes].astype(F32) for t in range(3)]
        columns = queries.T.astype(BF16)
        arrive(2 * h)
        for row in range(0, rows, 2):
            spread = jnp.dot(columns, masks[row // 2], preferred_element_type=F32)
            for u in range(2):
                raw_ref[row + u : row + u + 1, :] = jnp.sum(
                    spread[:, u * dim : (u + 1) * dim] * state_ref[row + u, h],
                    axis=0, keepdims=True,
                )
        retain = jnp.exp(jnp.full((1, dim), -decay_ref[h], F32))
        flat = retain * raw_ref[...] + jnp.sum(queries * keys, axis=1, keepdims=True) * values
        squares += jnp.sum(flat * flat, axis=1, keepdims=True)
        scaled = (flat * attn_gain_ref[lanes].reshape(1, dim)).astype(BF16)
        arrive(2 * h + 1)
        term = jnp.dot(scaled, weight_ref[lanes, :], preferred_element_type=F32)
        if h == 0:
            acc_ref[...] = term
        else:
            acc_ref[...] += term

    square_row = jnp.broadcast_to(squares, (rows, LANES)).T[0:1, :]
    square_row = jnp.concatenate([square_row, jnp.zeros((1, LANES - rows), F32)], axis=1)
    pieces = list(split_terms(square_row))
    for j in range(width // LANES):
        pieces += list(split_terms(moe_gain_ref[j * LANES : (j + 1) * LANES].reshape(1, LANES)))
    pieces.append(jnp.zeros((rows - len(pieces), LANES), F32))
    beside = jnp.concatenate(pieces, axis=0).astype(BF16)
    for target in range(out_ref.shape[0]):
        out_ref[target, :, :width] = acc_ref[:, target * width : (target + 1) * width].astype(BF16)
        out_ref[target, :, width:] = beside


def update_kernel(decay_ref, qkv_ref, state_ref, after_ref, out_ref):
    del after_ref
    head = pl.program_id(0)
    rows, dim = qkv_ref.shape[1:]
    columns = qkv_ref[1].astype(F32).T.astype(BF16)
    values = qkv_ref[2].astype(F32)
    values = jnp.concatenate([values, values], axis=1)
    retain = jnp.exp(jnp.full((1, dim), -decay_ref[head], F32))
    for row in range(0, rows, 2):
        picked = jnp.where(row_pair_mask(row, rows, dim), values, 0.0).astype(BF16)
        outer = jnp.dot(columns, picked, preferred_element_type=F32)
        for u in range(2):
            out_ref[row + u, 0] = (
                retain * state_ref[row + u, 0] + outer[:, u * dim : (u + 1) * dim]
            )


def as_columns(table):
    rows = table.shape[1]
    padded = [table.astype(F32), jnp.zeros((8 - table.shape[0], rows), F32)]
    return jnp.concatenate(padded, axis=0).T


def slot_masks(table, rows, slots):
    ids = as_columns(table)
    lane = lax.broadcasted_iota(jnp.int32, (rows, slots), 1)
    expert, place = lane // CAP, lane % CAP
    named = [(ids[:, c : c + 1] == expert.astype(F32)) for c in range(table.shape[0])]
    total = sum(n.astype(F32) for n in named)
    before = (
        lax.broadcasted_iota(jnp.int32, (rows, rows), 1)
        < lax.broadcasted_iota(jnp.int32, (rows, rows), 0)
    ).astype(BF16)
    earlier = jnp.dot(before, total.astype(BF16), preferred_element_type=F32)
    here = earlier == place.astype(F32)
    return [(n & here).astype(F32) for n in named]


def dispatch_kernel(
    parts_ref, resid_ref, ids_ref, state_hbm, weight_hbm, out_ref, hidden_ref, gain_ref, *, features, slots,
):
    del state_hbm, weight_hbm
    sources, rows, _ = parts_ref.shape
    width = resid_ref.shape[1]
    total = jnp.zeros((rows, width), F32)
    beside = jnp.zeros((1, LANES), F32)
    for s in range(sources):
        total += parts_ref[s, :, :width].astype(F32)
        extra = parts_ref[s, :, width:].astype(F32)
        beside += jnp.sum(extra[0:3], axis=0, keepdims=True)
        for j in range(width // LANES):
            gain_ref[:, s * width + j * LANES : s * width + (j + 1) * LANES] = jnp.sum(
                extra[3 + 3 * j : 6 + 3 * j], axis=0, keepdims=True
            )
    squares = jnp.broadcast_to(beside, (LANES, LANES)).T[:rows, 0:1]
    hidden = resid_ref[...].astype(F32) + total * lax.rsqrt(squares / features + EPS)
    hidden_ref[...] = hidden
    placing = sum(slot_masks(ids_ref[...], rows, slots)).astype(BF16)
    buckets = lax.dot_general(
        placing, hidden.astype(BF16), (((0,), (0,)), ((), ())), preferred_element_type=F32
    ).astype(BF16)
    side, grp, head, per_target, _ = out_ref.shape
    for g in range(grp):
        block = buckets[g * per_target : (g + 1) * per_target]
        for s in range(side):
            for h in range(head):
                out_ref[s, g, h] = block


def expert_kernel(
    rows_ref, gain_ref, gate_up_ref, down_ref, out_hbm, mixed_ref, held_ref, out_ref, out_sem
):
    experts = gate_up_ref.shape[0]
    side, grp, head, per_target, width = rows_ref.shape
    model = head * width
    count = side * grp * CAP
    squares = jnp.zeros((side * grp, per_target, 1), F32)
    for h in range(head):
        rows = rows_ref[:, :, h].reshape(side * grp, per_target, width).astype(F32)
        squares += jnp.sum(rows * rows, axis=2, keepdims=True)
        mixed = rows * gain_ref[:, h * width : (h + 1) * width].reshape(1, 1, width)
        for e in range(experts):
            mixed_ref[e, :, h * width : (h + 1) * width] = (
                mixed[:, e * CAP : (e + 1) * CAP].reshape(count, width).astype(BF16)
            )
    scale = lax.rsqrt(squares / model + EPS)
    sends = []
    for e in range(experts):
        row_scale = scale[:, e * CAP : (e + 1) * CAP].reshape(count, 1)
        contract = (((1,), (1,)), ((), ()))
        gate = row_scale * lax.dot_general(
            mixed_ref[e], gate_up_ref[e, 0], contract, preferred_element_type=F32
        )
        up = row_scale * lax.dot_general(
            mixed_ref[e], gate_up_ref[e, 1], contract, preferred_element_type=F32
        )
        activated = (gate / (1.0 + jnp.exp(-gate)) * up).astype(BF16)
        for h in range(head):
            held_ref[:, h, e * CAP : (e + 1) * CAP, :] = jnp.dot(
                activated,
                down_ref[e, :, h * width : (h + 1) * width],
                preferred_element_type=F32,
            ).reshape(side * grp, CAP, width)
            if e == experts - 1:
                block = held_ref[:, h].astype(BF16)
                out_ref[:, :, h] = block.reshape(side, grp, per_target, width)
                sends.append(
                    pltpu.make_async_copy(out_ref.at[:, :, h], out_hbm.at[:, :, h], out_sem.at[h])
                )
                sends[-1].start()
    for send in sends:
        send.wait()


def combine_kernel(parts_ref, hidden_ref, ids_ref, bins_ref, out_ref):
    side, grp, head, per_target, width = parts_ref.shape
    rows = hidden_ref.shape[0]
    total = jnp.zeros((grp, per_target, width), F32)
    for s in range(side):
        for h in range(head):
            total += parts_ref[s, :, h].astype(F32)
    slots = grp * per_target
    expert_out = total.reshape(slots, width).astype(BF16)
    bins = as_columns(bins_ref[...])
    weight = bins / jnp.sum(bins, axis=1, keepdims=True)
    routed = jnp.zeros((rows, width), F32)
    for c, mask in enumerate(slot_masks(ids_ref[...], rows, slots)):
        picked = jnp.dot(mask.astype(BF16), expert_out, preferred_element_type=F32)
        routed += weight[:, c : c + 1] * picked
    out_ref[...] = (hidden_ref[...] + routed).astype(BF16)


def in_hbm(*arrays):
    return [pltpu.with_memory_space_constraint(array, pltpu.HBM) for array in arrays]


def on_device(
    qkv, state, decay_rate, attn_gain, out_weight, resid, moe_gain, expert_ids, gate_bins,
    gate_up, down,
):
    rows, heads, head_dim, _ = state.shape
    side, grp, head = lax.axis_size("side"), lax.axis_size("grp"), lax.axis_size("head")
    width = resid.shape[1]
    model = width * head
    experts = gate_up.shape[0]
    slots = experts * grp * CAP
    vmem, hbm = pl.BlockSpec(memory_space=pltpu.VMEM), pl.BlockSpec(memory_space=pltpu.HBM)
    smem = pl.BlockSpec(memory_space=pltpu.SMEM)
    params = pltpu.CompilerParams(vmem_limit_bytes=24 * MIB)
    qkv = jnp.transpose(qkv, (1, 0, 2))
    expert_ids, gate_bins = expert_ids.T, gate_bins.T
    partial, held_resid = pl.pallas_call(
        readout_kernel,
        in_specs=[smem, hbm, hbm, vmem, hbm, vmem, vmem],
        out_specs=[vmem, vmem],
        out_shape=[
            jax.ShapeDtypeStruct((head, rows, width + LANES), BF16),
            jax.ShapeDtypeStruct((rows, width), BF16),
        ],
        scratch_shapes=[
            pltpu.VMEM(qkv.shape, BF16),
            pltpu.VMEM(state.shape, F32),
            pltpu.VMEM(out_weight.shape, BF16),
            pltpu.VMEM((rows, head_dim), F32),
            pltpu.VMEM((rows, model), F32),
            pltpu.SemaphoreType.DMA((1,)),
            pltpu.SemaphoreType.DMA((heads,)),
            pltpu.SemaphoreType.DMA((heads,)),
        ],
        compiler_params=params,
        name="readout",
    )(
        *in_hbm(decay_rate, qkv, state, attn_gain, out_weight, moe_gain, resid)
    )
    parts = lax.all_to_all(partial, "head", 0, 0, tiled=True)

    outgoing, hidden, gain = pl.pallas_call(
        functools.partial(dispatch_kernel, features=heads * head_dim * head, slots=slots),
        in_specs=[vmem] * 3 + [hbm] * 2,
        out_specs=[vmem] * 3,
        out_shape=[
            jax.ShapeDtypeStruct((side, grp, head, experts * CAP, width), BF16),
            jax.ShapeDtypeStruct((rows, width), F32),
            jax.ShapeDtypeStruct((1, model), F32),
        ],
        compiler_params=params,
        name="dispatch",
    )(parts, held_resid, expert_ids, *in_hbm(state, out_weight))
    everyone = ("side", "grp", "head")
    block = (side * grp * head, experts * CAP, width)
    arrived = lax.all_to_all(outgoing.reshape(block), everyone, 0, 0, tiled=True)

    new_state = pl.pallas_call(
        update_kernel,
        grid=(heads,),
        in_specs=[
            smem,
            pl.BlockSpec((3, rows, head_dim), lambda h: (0, 0, h)),
            pl.BlockSpec((rows, 1, head_dim, head_dim), lambda h: (0, h, 0, 0)),
            pl.BlockSpec(memory_space=pl.ANY),
        ],
        out_specs=pl.BlockSpec((rows, 1, head_dim, head_dim), lambda h: (0, h, 0, 0)),
        out_shape=jax.ShapeDtypeStruct(state.shape, F32),
        compiler_params=params,
        cost_estimate=pl.CostEstimate(
            flops=4 * state.size, bytes_accessed=8 * state.size, transcendentals=0
        ),
        name="update",
    )(*in_hbm(decay_rate, qkv, state), hidden)

    expert_out = pl.pallas_call(
        expert_kernel,
        in_specs=[vmem] * 4,
        out_specs=hbm,
        out_shape=jax.ShapeDtypeStruct((side, grp, head, experts * CAP, width), BF16),
        scratch_shapes=[
            pltpu.VMEM((experts, side * grp * CAP, model), BF16),
            pltpu.VMEM((side * grp, head, experts * CAP, width), F32),
            pltpu.VMEM((side, grp, head, experts * CAP, width), BF16),
            pltpu.SemaphoreType.DMA((head,)),
        ],
        compiler_params=params,
        name="experts",
    )(
        arrived.reshape(side, grp, head, experts * CAP, width), gain,
        pltpu.with_memory_space_constraint(gate_up, pltpu.VMEM),
        pltpu.with_memory_space_constraint(down, pltpu.VMEM),
    )
    returned = lax.all_to_all(expert_out.reshape(block), everyone, 0, 0, tiled=True)

    layer_out = pl.pallas_call(
        combine_kernel,
        in_specs=[vmem] * 4,
        out_specs=vmem,
        out_shape=jax.ShapeDtypeStruct((rows, width), BF16),
        compiler_params=params,
        name="combine",
    )(returned.reshape(side, grp, head, experts * CAP, width), hidden, expert_ids, gate_bins)
    return new_state, layer_out


def solution(mesh):
    placed = (
        P(("side", "grp"), None, "head"),
        P(("side", "grp"), "head", None, None),
        P("head"),
        P("head"),
        P("head", None),
        P(("side", "grp"), "head"),
        P("head"),
        P(("side", "grp"), None),
        P(("side", "grp"), None),
        P("grp", None, ("side", "head"), None),
        P("grp", ("side", "head"), None),
    )
    return jax.shard_map(
        on_device,
        mesh=mesh,
        in_specs=placed,
        out_specs=(P(("side", "grp"), "head", None, None), P(("side", "grp"), "head")),
        check_vma=False,
    )
```

```python
import functools

import jax
import jax.numpy as jnp
from jax import lax
from jax.experimental import pallas as pl
from jax.experimental.pallas import tpu as pltpu
from jax.sharding import PartitionSpec as P

CAP = 8
EPS = 1e-06
LANES = 128
IN_FLIGHT = 5
F32 = jnp.float32
BF16 = jnp.bfloat16
MIB = 1024 * 1024


def split_terms(value):
    first = value.astype(BF16).astype(F32)
    rest = value - first
    second = rest.astype(BF16).astype(F32)
    third = (rest - second).astype(BF16).astype(F32)
    return first, second, third


def row_pair_mask(row, rows, dim):
    i = lax.broadcasted_iota(jnp.int32, (rows, 2 * dim), 0)
    j = lax.broadcasted_iota(jnp.int32, (rows, 2 * dim), 1)
    return i == row + (j >= dim).astype(jnp.int32)


def as_columns(table):
    rows = table.shape[1]
    padded = [table.astype(F32), jnp.zeros((8 - table.shape[0], rows), F32)]
    return jnp.concatenate(padded, axis=0).T


def slot_masks(table, rows, slots):
    ids = as_columns(table)
    lane = lax.broadcasted_iota(jnp.int32, (rows, slots), 1)
    expert, place = lane // CAP, lane % CAP
    named = [(ids[:, c : c + 1] == expert.astype(F32)) for c in range(table.shape[0])]
    total = sum(n.astype(F32) for n in named)
    before = (
        lax.broadcasted_iota(jnp.int32, (rows, rows), 1)
        < lax.broadcasted_iota(jnp.int32, (rows, rows), 0)
    ).astype(BF16)
    earlier = jnp.dot(before, total.astype(BF16), preferred_element_type=F32)
    here = earlier == place.astype(F32)
    return [(n & here).astype(F32) for n in named]


def readout_kernel(
    decay_hbm, qkv_hbm, state_hbm, attn_gain_hbm, weight_hbm, moe_gain_hbm, resid_hbm, ids_hbm, bins_hbm,
    out_ref, resid_ref, picks_ref, share_ref,
    decay_ref, qkv_ref, state_ref, attn_gain_ref, weight_ref, moe_gain_ref, ids_ref, bins_ref,
    raw_ref, acc_ref, small_sem, state_sem, weight_sem,
):
    rows, heads, dim, _ = state_ref.shape
    width = moe_gain_ref.shape[0]
    small = [
        pltpu.make_async_copy(source, target, small_sem.at[i])
        for i, (source, target) in enumerate(
            (
                (qkv_hbm, qkv_ref), (decay_hbm, decay_ref), (attn_gain_hbm, attn_gain_ref),
                (ids_hbm, ids_ref), (bins_hbm, bins_ref), (moe_gain_hbm, moe_gain_ref),
                (resid_hbm, resid_ref),
            )
        )
    ]
    loads = []
    for h in range(heads):
        span = pl.ds(h * dim, dim)
        loads.append(
            pltpu.make_async_copy(weight_hbm.at[span], weight_ref.at[span], weight_sem.at[h])
        )
        loads.append(
            pltpu.make_async_copy(state_hbm.at[:, h], state_ref.at[:, h], state_sem.at[h])
        )
    for copy in small:
        copy.start()
    for load in loads[:IN_FLIGHT]:
        load.start()

    def arrive(index):
        loads[index].wait()
        if index + IN_FLIGHT < len(loads):
            loads[index + IN_FLIGHT].start()

    masks = [row_pair_mask(row, rows, dim).astype(BF16) for row in range(0, rows, 2)]
    for copy in small:
        copy.wait()
    for c, mask in enumerate(slot_masks(ids_ref[...], rows, picks_ref.shape[2])):
        picks_ref[c] = mask.astype(BF16)
    bins = as_columns(bins_ref[...])
    share_ref[...] = bins / jnp.sum(bins, axis=1, keepdims=True)
    squares = jnp.zeros((rows, 1), F32)
    for h in range(heads):
        lanes = slice(h * dim, (h + 1) * dim)
        queries, keys, values = [qkv_ref[t, :, lanes].astype(F32) for t in range(3)]
        columns = queries.T.astype(BF16)
        arrive(2 * h)
        arrive(2 * h + 1)
        for row in range(0, rows, 2):
            spread = jnp.dot(columns, masks[row // 2], preferred_element_type=F32)
            for u in range(2):
                raw_ref[row + u : row + u + 1, :] = jnp.sum(
                    spread[:, u * dim : (u + 1) * dim] * state_ref[row + u, h],
                    axis=0, keepdims=True,
                )
        retain = jnp.exp(jnp.full((1, dim), -decay_ref[h], F32))
        flat = retain * raw_ref[...] + jnp.sum(queries * keys, axis=1, keepdims=True) * values
        squares += jnp.sum(flat * flat, axis=1, keepdims=True)
        scaled = (flat * attn_gain_ref[lanes].reshape(1, dim)).astype(BF16)
        term = jnp.dot(scaled, weight_ref[lanes, :], preferred_element_type=F32)
        if h == 0:
            acc_ref[...] = term
        else:
            acc_ref[...] += term

    square_row = jnp.broadcast_to(squares, (rows, LANES)).T[0:1, :]
    square_row = jnp.concatenate([square_row, jnp.zeros((1, LANES - rows), F32)], axis=1)
    pieces = list(split_terms(square_row))
    for j in range(width // LANES):
        pieces += list(split_terms(moe_gain_ref[j * LANES : (j + 1) * LANES].reshape(1, LANES)))
    pieces.append(jnp.zeros((rows - len(pieces), LANES), F32))
    beside = jnp.concatenate(pieces, axis=0).astype(BF16)
    for target in range(out_ref.shape[0]):
        out_ref[target, :, :width] = acc_ref[:, target * width : (target + 1) * width].astype(BF16)
        out_ref[target, :, width:] = beside


def update_kernel(decay_ref, qkv_ref, state_ref, after_ref, out_ref):
    del after_ref
    head = pl.program_id(0)
    rows, dim = qkv_ref.shape[1:]
    columns = qkv_ref[1].astype(F32).T.astype(BF16)
    values = qkv_ref[2].astype(F32)
    values = jnp.concatenate([values, values], axis=1)
    retain = jnp.exp(jnp.full((1, dim), -decay_ref[head], F32))
    for row in range(0, rows, 2):
        picked = jnp.where(row_pair_mask(row, rows, dim), values, 0.0).astype(BF16)
        outer = jnp.dot(columns, picked, preferred_element_type=F32)
        for u in range(2):
            out_ref[row + u, 0] = (
                retain * state_ref[row + u, 0] + outer[:, u * dim : (u + 1) * dim]
            )


def dispatch_kernel(
    parts_ref, resid_ref, picks_ref, state_hbm, weight_hbm, out_ref, hidden_ref, gain_ref, *, features,
):
    del state_hbm, weight_hbm
    sources, rows, _ = parts_ref.shape
    width = resid_ref.shape[1]
    total = jnp.zeros((rows, width), F32)
    beside = jnp.zeros((1, LANES), F32)
    for s in range(sources):
        total += parts_ref[s, :, :width].astype(F32)
        extra = parts_ref[s, :, width:].astype(F32)
        beside += jnp.sum(extra[0:3], axis=0, keepdims=True)
        for j in range(width // LANES):
            gain_ref[:, s * width + j * LANES : s * width + (j + 1) * LANES] = jnp.sum(
                extra[3 + 3 * j : 6 + 3 * j], axis=0, keepdims=True
            )
    squares = jnp.broadcast_to(beside, (LANES, LANES)).T[:rows, 0:1]
    hidden = resid_ref[...].astype(F32) + total * lax.rsqrt(squares / features + EPS)
    hidden_ref[...] = hidden
    placing = sum(picks_ref[c] for c in range(picks_ref.shape[0]))
    buckets = lax.dot_general(
        placing, hidden.astype(BF16), (((0,), (0,)), ((), ())), preferred_element_type=F32
    ).astype(BF16)
    side, grp, head, per_target, _ = out_ref.shape
    for g in range(grp):
        block = buckets[g * per_target : (g + 1) * per_target]
        for s in range(side):
            for h in range(head):
                out_ref[s, g, h] = block


def expert_kernel(
    rows_ref, gain_ref, gate_up_ref, down_ref, out_hbm, mixed_ref, held_ref, out_ref, out_sem
):
    experts = gate_up_ref.shape[0]
    side, grp, head, per_target, width = rows_ref.shape
    model = head * width
    count = side * grp * CAP
    squares = jnp.zeros((side * grp, per_target, 1), F32)
    for h in range(head):
        rows = rows_ref[:, :, h].reshape(side * grp, per_target, width).astype(F32)
        squares += jnp.sum(rows * rows, axis=2, keepdims=True)
        mixed = rows * gain_ref[:, h * width : (h + 1) * width].reshape(1, 1, width)
        for e in range(experts):
            mixed_ref[e, :, h * width : (h + 1) * width] = (
                mixed[:, e * CAP : (e + 1) * CAP].reshape(count, width).astype(BF16)
            )
    scale = lax.rsqrt(squares / model + EPS)
    sends = []
    for e in range(experts):
        row_scale = scale[:, e * CAP : (e + 1) * CAP].reshape(count, 1)
        contract = (((1,), (1,)), ((), ()))
        gate = row_scale * lax.dot_general(
            mixed_ref[e], gate_up_ref[e, 0], contract, preferred_element_type=F32
        )
        up = row_scale * lax.dot_general(
            mixed_ref[e], gate_up_ref[e, 1], contract, preferred_element_type=F32
        )
        activated = (gate / (1.0 + jnp.exp(-gate)) * up).astype(BF16)
        for h in range(head):
            held_ref[:, h, e * CAP : (e + 1) * CAP, :] = jnp.dot(
                activated,
                down_ref[e, :, h * width : (h + 1) * width],
                preferred_element_type=F32,
            ).reshape(side * grp, CAP, width)
            if e == experts - 1:
                block = held_ref[:, h].astype(BF16)
                out_ref[:, :, h] = block.reshape(side, grp, per_target, width)
                sends.append(
                    pltpu.make_async_copy(out_ref.at[:, :, h], out_hbm.at[:, :, h], out_sem.at[h])
                )
                sends[-1].start()
    for send in sends:
        send.wait()


def combine_kernel(parts_ref, hidden_ref, picks_ref, share_ref, out_ref, slots_ref):
    side, grp, head, per_target, _ = parts_ref.shape
    for g in range(grp):
        total = parts_ref[0, g, 0].astype(F32)
        for i in range(1, side * head):
            total += parts_ref[i // head, g, i % head].astype(F32)
        slots_ref[g * per_target : (g + 1) * per_target] = total.astype(BF16)
    routed = jnp.zeros(hidden_ref.shape, F32)
    for c in range(picks_ref.shape[0]):
        picked = jnp.dot(picks_ref[c], slots_ref[...], preferred_element_type=F32)
        routed += share_ref[:, c : c + 1] * picked
    out_ref[...] = (hidden_ref[...] + routed).astype(BF16)


def in_hbm(*arrays):
    return [pltpu.with_memory_space_constraint(array, pltpu.HBM) for array in arrays]


def on_device(
    qkv, state, decay_rate, attn_gain, out_weight, resid, moe_gain, expert_ids, gate_bins,
    gate_up, down,
):
    rows, heads, head_dim, _ = state.shape
    side, grp, head = lax.axis_size("side"), lax.axis_size("grp"), lax.axis_size("head")
    width = resid.shape[1]
    model = width * head
    experts = gate_up.shape[0]
    slots = experts * grp * CAP
    vmem, hbm = pl.BlockSpec(memory_space=pltpu.VMEM), pl.BlockSpec(memory_space=pltpu.HBM)
    smem = pl.BlockSpec(memory_space=pltpu.SMEM)
    params = pltpu.CompilerParams(vmem_limit_bytes=24 * MIB)
    qkv = jnp.transpose(qkv, (1, 0, 2))
    expert_ids, gate_bins = expert_ids.T, gate_bins.T
    operands = (
        decay_rate, qkv, state, attn_gain, out_weight, moe_gain, resid, expert_ids, gate_bins,
    )
    partial, held_resid, picks, share = pl.pallas_call(
        readout_kernel,
        in_specs=[hbm] * len(operands),
        out_specs=[vmem] * 4,
        out_shape=[
            jax.ShapeDtypeStruct((head, rows, width + LANES), BF16),
            jax.ShapeDtypeStruct((rows, width), BF16),
            jax.ShapeDtypeStruct((expert_ids.shape[0], rows, slots), BF16),
            jax.ShapeDtypeStruct((rows, 8), F32),
        ],
        scratch_shapes=[
            pltpu.SMEM(decay_rate.shape, F32),
            pltpu.VMEM(qkv.shape, BF16),
            pltpu.VMEM(state.shape, F32),
            pltpu.VMEM(attn_gain.shape, F32),
            pltpu.VMEM(out_weight.shape, BF16),
            pltpu.VMEM(moe_gain.shape, F32),
            pltpu.VMEM(expert_ids.shape, jnp.int32),
            pltpu.VMEM(gate_bins.shape, jnp.int32),
            pltpu.VMEM((rows, head_dim), F32),
            pltpu.VMEM((rows, model), F32),
            pltpu.SemaphoreType.DMA((7,)),
            pltpu.SemaphoreType.DMA((heads,)),
            pltpu.SemaphoreType.DMA((heads,)),
        ],
        compiler_params=params,
        name="readout",
    )(*in_hbm(*operands))
    parts = lax.all_to_all(partial, "head", 0, 0, tiled=True)

    outgoing, hidden, gain = pl.pallas_call(
        functools.partial(dispatch_kernel, features=heads * head_dim * head),
        in_specs=[vmem] * 3 + [hbm] * 2,
        out_specs=[vmem] * 3,
        out_shape=[
            jax.ShapeDtypeStruct((side, grp, head, experts * CAP, width), BF16),
            jax.ShapeDtypeStruct((rows, width), F32),
            jax.ShapeDtypeStruct((1, model), F32),
        ],
        compiler_params=params,
        name="dispatch",
    )(parts, held_resid, picks, *in_hbm(state, out_weight))
    everyone = ("side", "grp", "head")
    block = (side * grp * head, experts * CAP, width)
    arrived = lax.all_to_all(outgoing.reshape(block), everyone, 0, 0, tiled=True)

    new_state = pl.pallas_call(
        update_kernel,
        grid=(heads,),
        in_specs=[
            smem,
            pl.BlockSpec((3, rows, head_dim), lambda h: (0, 0, h)),
            pl.BlockSpec((rows, 1, head_dim, head_dim), lambda h: (0, h, 0, 0)),
            pl.BlockSpec(memory_space=pl.ANY),
        ],
        out_specs=pl.BlockSpec((rows, 1, head_dim, head_dim), lambda h: (0, h, 0, 0)),
        out_shape=jax.ShapeDtypeStruct(state.shape, F32),
        compiler_params=params,
        cost_estimate=pl.CostEstimate(
            flops=4 * state.size, bytes_accessed=8 * state.size, transcendentals=0
        ),
        name="update",
    )(*in_hbm(decay_rate, qkv, state), hidden)

    expert_out = pl.pallas_call(
        expert_kernel,
        in_specs=[vmem] * 4,
        out_specs=hbm,
        out_shape=jax.ShapeDtypeStruct((side, grp, head, experts * CAP, width), BF16),
        scratch_shapes=[
            pltpu.VMEM((experts, side * grp * CAP, model), BF16),
            pltpu.VMEM((side * grp, head, experts * CAP, width), F32),
            pltpu.VMEM((side, grp, head, experts * CAP, width), BF16),
            pltpu.SemaphoreType.DMA((head,)),
        ],
        compiler_params=params,
        name="experts",
    )(
        arrived.reshape(side, grp, head, experts * CAP, width), gain,
        pltpu.with_memory_space_constraint(gate_up, pltpu.VMEM),
        pltpu.with_memory_space_constraint(down, pltpu.VMEM),
    )
    returned = lax.all_to_all(expert_out.reshape(block), everyone, 0, 0, tiled=True)

    layer_out = pl.pallas_call(
        combine_kernel,
        in_specs=[vmem] * 4,
        out_specs=vmem,
        out_shape=jax.ShapeDtypeStruct((rows, width), BF16),
        scratch_shapes=[pltpu.VMEM((slots, width), BF16)],
        compiler_params=params,
        name="combine",
    )(returned.reshape(side, grp, head, experts * CAP, width), hidden, picks, share)
    return new_state, layer_out


def solution(mesh):
    placed = (
        P(("side", "grp"), None, "head"),
        P(("side", "grp"), "head", None, None),
        P("head"),
        P("head"),
        P("head", None),
        P(("side", "grp"), "head"),
        P("head"),
        P(("side", "grp"), None),
        P(("side", "grp"), None),
        P("grp", None, ("side", "head"), None),
        P("grp", ("side", "head"), None),
    )
    return jax.shard_map(
        on_device,
        mesh=mesh,
        in_specs=placed,
        out_specs=(P(("side", "grp"), "head", None, None), P(("side", "grp"), "head")),
        check_vma=False,
    )
```

```python
import functools

import jax
import jax.numpy as jnp
from jax import lax
from jax.experimental import pallas as pl
from jax.experimental.pallas import tpu as pltpu
from jax.sharding import PartitionSpec as P

CAP = 8
EPS = 1e-06
LANES = 128
BESIDE = 16
IN_FLIGHT = 5
F32 = jnp.float32
BF16 = jnp.bfloat16
MIB = 1024 * 1024


def split_terms(value):
    first = value.astype(BF16).astype(F32)
    rest = value - first
    second = rest.astype(BF16).astype(F32)
    third = (rest - second).astype(BF16).astype(F32)
    return first, second, third


def row_pair_mask(row, rows, dim):
    i = lax.broadcasted_iota(jnp.int32, (rows, 2 * dim), 0)
    j = lax.broadcasted_iota(jnp.int32, (rows, 2 * dim), 1)
    return i == row + (j >= dim).astype(jnp.int32)


def as_columns(table):
    rows = table.shape[1]
    padded = [table.astype(F32), jnp.zeros((8 - table.shape[0], rows), F32)]
    return jnp.concatenate(padded, axis=0).T


def slot_masks(table, rows, slots):
    ids = as_columns(table)
    lane = lax.broadcasted_iota(jnp.int32, (rows, slots), 1)
    expert, place = lane // CAP, lane % CAP
    named = [(ids[:, c : c + 1] == expert.astype(F32)) for c in range(table.shape[0])]
    total = sum(n.astype(F32) for n in named)
    before = (
        lax.broadcasted_iota(jnp.int32, (rows, rows), 1)
        < lax.broadcasted_iota(jnp.int32, (rows, rows), 0)
    ).astype(BF16)
    earlier = jnp.dot(before, total.astype(BF16), preferred_element_type=F32)
    here = earlier == place.astype(F32)
    return [(n & here).astype(F32) for n in named]


def readout_kernel(
    decay_hbm, qkv_hbm, state_hbm, attn_gain_hbm, weight_hbm, moe_gain_hbm, resid_hbm, ids_hbm, bins_hbm,
    out_ref, resid_ref, picks_ref, share_ref,
    decay_ref, qkv_ref, state_ref, attn_gain_ref, weight_ref, moe_gain_ref, ids_ref, bins_ref,
    raw_ref, acc_ref, beside_ref, small_sem, state_sem, weight_sem,
):
    rows, heads, dim, _ = state_ref.shape
    width = moe_gain_ref.shape[0]
    small = [
        pltpu.make_async_copy(source, target, small_sem.at[i])
        for i, (source, target) in enumerate(
            (
                (qkv_hbm, qkv_ref), (decay_hbm, decay_ref), (attn_gain_hbm, attn_gain_ref),
                (ids_hbm, ids_ref), (bins_hbm, bins_ref), (moe_gain_hbm, moe_gain_ref),
                (resid_hbm, resid_ref),
            )
        )
    ]
    loads = []
    for h in range(heads):
        span = pl.ds(h * dim, dim)
        loads.append(
            pltpu.make_async_copy(weight_hbm.at[span], weight_ref.at[span], weight_sem.at[h])
        )
        parts = 2 if h == heads - 1 else 1
        for p in range(parts):
            view = (pl.ds(p * (rows // parts), rows // parts), h)
            loads.append(
                pltpu.make_async_copy(
                    state_hbm.at[view], state_ref.at[view], state_sem.at[h + p]
                )
            )
    for copy in small:
        copy.start()
    for load in loads[:IN_FLIGHT]:
        load.start()

    def arrive(index):
        loads[index].wait()
        if index + IN_FLIGHT < len(loads):
            loads[index + IN_FLIGHT].start()

    masks = [row_pair_mask(row, rows, dim).astype(BF16) for row in range(0, rows, 2)]
    for copy in small:
        copy.wait()
    for c, mask in enumerate(slot_masks(ids_ref[...], rows, picks_ref.shape[2])):
        picks_ref[c] = mask.astype(BF16)
    pieces = [jnp.zeros((3, LANES), F32)]
    for j in range(width // LANES):
        pieces += list(split_terms(moe_gain_ref[j * LANES : (j + 1) * LANES].reshape(1, LANES)))
    pieces.append(jnp.zeros((BESIDE - 3 - 3 * (width // LANES), LANES), F32))
    beside_ref[...] = jnp.concatenate(pieces, axis=0)
    bins = as_columns(bins_ref[...])
    share_ref[...] = bins / jnp.sum(bins, axis=1, keepdims=True)
    squares = jnp.zeros((rows, 1), F32)
    for h in range(heads):
        lanes = slice(h * dim, (h + 1) * dim)
        queries, keys, values = [qkv_ref[t, :, lanes].astype(F32) for t in range(3)]
        columns = queries.T.astype(BF16)
        arrive(2 * h)
        arrive(2 * h + 1)
        for row in range(0, rows, 2):
            if h == heads - 1 and row == rows // 2:
                arrive(2 * h + 2)
            spread = jnp.dot(columns, masks[row // 2], preferred_element_type=F32)
            for u in range(2):
                raw_ref[row + u : row + u + 1, :] = jnp.sum(
                    spread[:, u * dim : (u + 1) * dim] * state_ref[row + u, h],
                    axis=0, keepdims=True,
                )
        retain = jnp.exp(jnp.full((1, dim), -decay_ref[h], F32))
        flat = retain * raw_ref[...] + jnp.sum(queries * keys, axis=1, keepdims=True) * values
        squares += jnp.sum(flat * flat, axis=1, keepdims=True)
        scaled = (flat * attn_gain_ref[lanes].reshape(1, dim)).astype(BF16)
        term = jnp.dot(scaled, weight_ref[lanes, :], preferred_element_type=F32)
        if h == 0:
            acc_ref[...] = term
        else:
            acc_ref[...] += term

    square_row = jnp.broadcast_to(squares, (rows, LANES)).T[0:1, :]
    square_row = jnp.concatenate([square_row, jnp.zeros((1, LANES - rows), F32)], axis=1)
    pieces = list(split_terms(square_row)) + [jnp.zeros((BESIDE - 3, LANES), F32)]
    beside = (beside_ref[...] + jnp.concatenate(pieces, axis=0)).astype(BF16)
    blocks = width // LANES
    for target in range(out_ref.shape[0]):
        for j in range(blocks):
            start = target * width + j * LANES
            out_ref[target, j * rows : (j + 1) * rows, :] = acc_ref[
                :, start : start + LANES
            ].astype(BF16)
        out_ref[target, blocks * rows :, :] = beside


def update_kernel(decay_ref, qkv_ref, state_ref, after_ref, out_ref):
    del after_ref
    head = pl.program_id(0)
    rows, dim = qkv_ref.shape[1:]
    columns = qkv_ref[1].astype(F32).T.astype(BF16)
    values = qkv_ref[2].astype(F32)
    values = jnp.concatenate([values, values], axis=1)
    retain = jnp.exp(jnp.full((1, dim), -decay_ref[head], F32))
    for row in range(0, rows, 2):
        picked = jnp.where(row_pair_mask(row, rows, dim), values, 0.0).astype(BF16)
        outer = jnp.dot(columns, picked, preferred_element_type=F32)
        for u in range(2):
            out_ref[row + u, 0] = (
                retain * state_ref[row + u, 0] + outer[:, u * dim : (u + 1) * dim]
            )


def dispatch_kernel(
    parts_ref, resid_ref, picks_ref, state_hbm, weight_hbm, out_ref, hidden_ref, gain_ref, *, features,
):
    del state_hbm, weight_hbm
    sources = parts_ref.shape[0]
    rows, width = resid_ref.shape
    blocks = width // LANES
    totals = [jnp.zeros((rows, LANES), F32)] * blocks
    beside = jnp.zeros((1, LANES), F32)
    for s in range(sources):
        for j in range(blocks):
            totals[j] += parts_ref[s, j * rows : (j + 1) * rows, :].astype(F32)
        extra = parts_ref[s, blocks * rows :, :].astype(F32)
        beside += jnp.sum(extra[0:3], axis=0, keepdims=True)
        for j in range(blocks):
            gain_ref[:, s * width + j * LANES : s * width + (j + 1) * LANES] = jnp.sum(
                extra[3 + 3 * j : 6 + 3 * j], axis=0, keepdims=True
            )
    squares = jnp.broadcast_to(beside, (LANES, LANES)).T[:rows, 0:1]
    total = jnp.concatenate(totals, axis=1)
    hidden = resid_ref[...].astype(F32) + total * lax.rsqrt(squares / features + EPS)
    hidden_ref[...] = hidden
    placing = sum(picks_ref[c] for c in range(picks_ref.shape[0]))
    buckets = lax.dot_general(
        placing, hidden.astype(BF16), (((0,), (0,)), ((), ())), preferred_element_type=F32
    ).astype(BF16)
    side, grp, head, per_target, _ = out_ref.shape
    for g in range(grp):
        block = buckets[g * per_target : (g + 1) * per_target]
        for s in range(side):
            for h in range(head):
                out_ref[s, g, h] = block


def expert_kernel(
    rows_ref, gain_ref, gate_up_ref, down_ref, out_hbm, mixed_ref, held_ref, out_ref, out_sem
):
    experts = gate_up_ref.shape[0]
    side, grp, head, per_target, width = rows_ref.shape
    model = head * width
    count = side * grp * CAP
    squares = jnp.zeros((side * grp, per_target, 1), F32)
    for h in range(head):
        rows = rows_ref[:, :, h].reshape(side * grp, per_target, width).astype(F32)
        squares += jnp.sum(rows * rows, axis=2, keepdims=True)
        mixed = rows * gain_ref[:, h * width : (h + 1) * width].reshape(1, 1, width)
        for e in range(experts):
            mixed_ref[e, :, h * width : (h + 1) * width] = (
                mixed[:, e * CAP : (e + 1) * CAP].reshape(count, width).astype(BF16)
            )
    scale = lax.rsqrt(squares / model + EPS)
    sends = []
    for e in range(experts):
        row_scale = scale[:, e * CAP : (e + 1) * CAP].reshape(count, 1)
        contract = (((1,), (1,)), ((), ()))
        gate = row_scale * lax.dot_general(
            mixed_ref[e], gate_up_ref[e, 0], contract, preferred_element_type=F32
        )
        up = row_scale * lax.dot_general(
            mixed_ref[e], gate_up_ref[e, 1], contract, preferred_element_type=F32
        )
        activated = (gate / (1.0 + jnp.exp(-gate)) * up).astype(BF16)
        for h in range(head):
            held_ref[:, h, e * CAP : (e + 1) * CAP, :] = jnp.dot(
                activated,
                down_ref[e, :, h * width : (h + 1) * width],
                preferred_element_type=F32,
            ).reshape(side * grp, CAP, width)
            if e == experts - 1:
                block = held_ref[:, h].astype(BF16)
                out_ref[:, :, h] = block.reshape(side, grp, per_target, width)
                sends.append(
                    pltpu.make_async_copy(out_ref.at[:, :, h], out_hbm.at[:, :, h], out_sem.at[h])
                )
                sends[-1].start()
    for send in sends:
        send.wait()


def combine_kernel(parts_ref, hidden_ref, picks_ref, share_ref, out_ref, slots_ref):
    side, grp, head, per_target, _ = parts_ref.shape
    for g in range(grp):
        total = parts_ref[0, g, 0].astype(F32)
        for i in range(1, side * head):
            total += parts_ref[i // head, g, i % head].astype(F32)
        slots_ref[g * per_target : (g + 1) * per_target] = total.astype(BF16)
    routed = jnp.zeros(hidden_ref.shape, F32)
    for c in range(picks_ref.shape[0]):
        picked = jnp.dot(picks_ref[c], slots_ref[...], preferred_element_type=F32)
        routed += share_ref[:, c : c + 1] * picked
    out_ref[...] = (hidden_ref[...] + routed).astype(BF16)


def in_hbm(*arrays):
    return [pltpu.with_memory_space_constraint(array, pltpu.HBM) for array in arrays]


def on_device(
    qkv, state, decay_rate, attn_gain, out_weight, resid, moe_gain, expert_ids, gate_bins,
    gate_up, down,
):
    rows, heads, head_dim, _ = state.shape
    side, grp, head = lax.axis_size("side"), lax.axis_size("grp"), lax.axis_size("head")
    width = resid.shape[1]
    model = width * head
    experts = gate_up.shape[0]
    slots = experts * grp * CAP
    vmem, hbm = pl.BlockSpec(memory_space=pltpu.VMEM), pl.BlockSpec(memory_space=pltpu.HBM)
    smem = pl.BlockSpec(memory_space=pltpu.SMEM)
    params = pltpu.CompilerParams(vmem_limit_bytes=24 * MIB)
    qkv = jnp.transpose(qkv, (1, 0, 2))
    expert_ids, gate_bins = expert_ids.T, gate_bins.T
    operands = (
        decay_rate, qkv, state, attn_gain, out_weight, moe_gain, resid, expert_ids, gate_bins,
    )
    partial, held_resid, picks, share = pl.pallas_call(
        readout_kernel,
        in_specs=[hbm] * len(operands),
        out_specs=[vmem] * 4,
        out_shape=[
            jax.ShapeDtypeStruct((head, rows * width // LANES + BESIDE, LANES), BF16),
            jax.ShapeDtypeStruct((rows, width), BF16),
            jax.ShapeDtypeStruct((expert_ids.shape[0], rows, slots), BF16),
            jax.ShapeDtypeStruct((rows, 8), F32),
        ],
        scratch_shapes=[
            pltpu.SMEM(decay_rate.shape, F32),
            pltpu.VMEM(qkv.shape, BF16),
            pltpu.VMEM(state.shape, F32),
            pltpu.VMEM(attn_gain.shape, F32),
            pltpu.VMEM(out_weight.shape, BF16),
            pltpu.VMEM(moe_gain.shape, F32),
            pltpu.VMEM(expert_ids.shape, jnp.int32),
            pltpu.VMEM(gate_bins.shape, jnp.int32),
            pltpu.VMEM((rows, head_dim), F32),
            pltpu.VMEM((rows, model), F32),
            pltpu.VMEM((BESIDE, LANES), F32),
            pltpu.SemaphoreType.DMA((7,)),
            pltpu.SemaphoreType.DMA((heads + 1,)),
            pltpu.SemaphoreType.DMA((heads,)),
        ],
        compiler_params=params,
        name="readout",
    )(*in_hbm(*operands))
    parts = lax.all_to_all(partial, "head", 0, 0, tiled=True)

    outgoing, hidden, gain = pl.pallas_call(
        functools.partial(dispatch_kernel, features=heads * head_dim * head),
        in_specs=[vmem] * 3 + [hbm] * 2,
        out_specs=[vmem] * 3,
        out_shape=[
            jax.ShapeDtypeStruct((side, grp, head, experts * CAP, width), BF16),
            jax.ShapeDtypeStruct((rows, width), F32),
            jax.ShapeDtypeStruct((1, model), F32),
        ],
        compiler_params=params,
        name="dispatch",
    )(parts, held_resid, picks, *in_hbm(state, out_weight))
    everyone = ("side", "grp", "head")
    block = (side * grp * head, experts * CAP, width)
    arrived = lax.all_to_all(outgoing.reshape(block), everyone, 0, 0, tiled=True)

    new_state = pl.pallas_call(
        update_kernel,
        grid=(heads,),
        in_specs=[
            smem,
            pl.BlockSpec((3, rows, head_dim), lambda h: (0, 0, h)),
            pl.BlockSpec((rows, 1, head_dim, head_dim), lambda h: (0, h, 0, 0)),
            pl.BlockSpec(memory_space=pl.ANY),
        ],
        out_specs=pl.BlockSpec((rows, 1, head_dim, head_dim), lambda h: (0, h, 0, 0)),
        out_shape=jax.ShapeDtypeStruct(state.shape, F32),
        compiler_params=params,
        cost_estimate=pl.CostEstimate(
            flops=4 * state.size, bytes_accessed=8 * state.size, transcendentals=0
        ),
        name="update",
    )(*in_hbm(decay_rate, qkv, state), hidden)

    expert_out = pl.pallas_call(
        expert_kernel,
        in_specs=[vmem] * 4,
        out_specs=hbm,
        out_shape=jax.ShapeDtypeStruct((side, grp, head, experts * CAP, width), BF16),
        scratch_shapes=[
            pltpu.VMEM((experts, side * grp * CAP, model), BF16),
            pltpu.VMEM((side * grp, head, experts * CAP, width), F32),
            pltpu.VMEM((side, grp, head, experts * CAP, width), BF16),
            pltpu.SemaphoreType.DMA((head,)),
        ],
        compiler_params=params,
        name="experts",
    )(
        arrived.reshape(side, grp, head, experts * CAP, width), gain,
        pltpu.with_memory_space_constraint(gate_up, pltpu.VMEM),
        pltpu.with_memory_space_constraint(down, pltpu.VMEM),
    )
    returned = lax.all_to_all(expert_out.reshape(block), everyone, 0, 0, tiled=True)

    layer_out = pl.pallas_call(
        combine_kernel,
        in_specs=[vmem] * 4,
        out_specs=vmem,
        out_shape=jax.ShapeDtypeStruct((rows, width), BF16),
        scratch_shapes=[pltpu.VMEM((slots, width), BF16)],
        compiler_params=params,
        name="combine",
    )(returned.reshape(side, grp, head, experts * CAP, width), hidden, picks, share)
    return new_state, layer_out


def solution(mesh):
    placed = (
        P(("side", "grp"), None, "head"),
        P(("side", "grp"), "head", None, None),
        P("head"),
        P("head"),
        P("head", None),
        P(("side", "grp"), "head"),
        P("head"),
        P(("side", "grp"), None),
        P(("side", "grp"), None),
        P("grp", None, ("side", "head"), None),
        P("grp", ("side", "head"), None),
    )
    return jax.shard_map(
        on_device,
        mesh=mesh,
        in_specs=placed,
        out_specs=(P(("side", "grp"), "head", None, None), P(("side", "grp"), "head")),
        check_vma=False,
    )
```
